256 devices in a mesh: dp: 8 (over x_hi, y), mp: 32 (over z, x_lo, core).
Axes of the slice: x: 4 (x_hi: 2, x_lo: 2; x = x_hi * 2 + x_lo), y: 4, z: 8, core: 2. Of those that a mesh axis runs over, the one named last changes fastest.
Arguments:
- tokens: bfloat16 [6144, 4096], P('dp', 'mp'), may hold values from -6 to 6
- cotangent: bfloat16 [6144, 4096], P('dp', 'mp'), may hold values from -6 to 6
- up_tiles: bfloat16 [384, 256, 256], P('mp'), may hold values from -0.1875 to 0.1875
- up_rows: int32 [384], P('mp'), may hold values from 0 to 15
- up_columns: int32 [384], P('mp'), may hold values from 0 to 63, as said below
- up_counts: int32 [32], P('mp'), may hold values from 6 to 12, as said below
- down_tiles: bfloat16 [384, 256, 256], P('mp'), may hold values from -0.09375 to 0.09375
- down_rows: int32 [384], P('mp'), may hold values from 0 to 63, as said below
- down_columns: int32 [384], P('mp'), may hold values from 0 to 15
- down_counts: int32 [32], P('mp'), may hold values from 6 to 12, as said below
Outputs:
- mixed: bfloat16 [6144, 4096], P('dp', 'mp')
- token_grads: bfloat16 [6144, 4096], P('dp', 'mp')
- up_grads: float32 [384, 256, 256], P('mp', 'dp')
- down_grads: float32 [384, 256, 256], P('mp', 'dp')
The draws below stay inside these ranges and needn't reach their ends.
Inputs may be any that keep to these rules, and one draw needn't show every extreme that they name: For the up slots of index j of mp, up_columns lies among that index's hidden blocks j * 2 to (j + 1) * 2 - 1; the live slots of one index name distinct blocks. `up_counts`: some index of mp has exactly 12 live up slots in every draw. For the down slots of index j of mp, down_rows lies among that index's hidden blocks j * 2 to (j + 1) * 2 - 1; the live slots of one index name distinct blocks. `down_counts`: some index of mp has exactly 12 live down slots in every draw.
All inputs are finite; a program needn't handle non-finite values.
Results may differ from the reference program's by a relative error of at most 0.023.
Values may be sent and summed in bfloat16 or wider, within the bound.
A program may use at most 128 MiB of HBM per device.

```python
import math
import jax
import jax.numpy as jnp
from jax import lax

D = 4096
FF = 16384
BLK = 256
TOKENS = 6144
DB = 16
HB = 2
MAXB = 12
N_MP = 32


def slot_pattern(key, salt):
    key = jax.random.fold_in(key, salt)
    count_key, pick_key, perm_key = jax.random.split(key, 3)
    counts = jax.random.randint(count_key, (N_MP,), MAXB // 2, MAXB + 1)
    chosen = jax.random.randint(pick_key, (), 0, N_MP)
    counts = jnp.where(jnp.arange(N_MP) == chosen, MAXB, counts).astype(jnp.int32)
    device_keys = jax.random.split(perm_key, N_MP)
    spots = jax.vmap(lambda item: jax.random.permutation(item, HB * DB)[:MAXB])(device_keys)
    places = jnp.arange(N_MP, dtype=jnp.int32)[:, None]
    hidden = (places * HB + spots // DB).reshape(-1).astype(jnp.int32)
    width = (spots % DB).reshape(-1).astype(jnp.int32)
    return (counts, hidden, width)


def draw_up_rows(key, part):
    return slot_pattern(key, 11)[2]


def draw_up_columns(key, part):
    return slot_pattern(key, 11)[1]


def draw_up_counts(key, part):
    return slot_pattern(key, 11)[0]


def draw_down_rows(key, part):
    return slot_pattern(key, 23)[1]


def draw_down_columns(key, part):
    return slot_pattern(key, 23)[2]


def draw_down_counts(key, part):
    return slot_pattern(key, 23)[0]


def steps_of(stream_key, shape, pieces, smallest, largest):
    def one(axis_at, shards_of):
        steps = jax.random.uniform(jax.random.fold_in(jax.random.fold_in(stream_key, 6), axis_at), (shards_of,), jnp.float32, smallest / len(pieces), largest / len(pieces))
        return jnp.repeat(jnp.exp(steps), shape[axis_at] // shards_of).reshape((-1,) + (1,) * (len(shape) - axis_at - 1))

    gain = one(*pieces[0])
    for cut in pieces[1:]:
        gain = gain * one(*cut)
    return gain


def gaussian(rng, shape, deviation, bound, shards=(), held_as=jnp.bfloat16):
    result = deviation * jax.random.normal(rng, shape, jnp.float32)
    if shards:
        result = result * steps_of(rng, shape, shards, -0.22, 0.18)
    return jnp.clip(result, -bound, bound).astype(held_as)


def setup_inputs(seed: int = 0) -> dict:
    splits = jax.random.split(jax.random.key(seed), 11)
    tokens = gaussian(splits[0], (TOKENS, D), 1.0, 6.0, ((0, 8), (1, 32)))
    cotangent = gaussian(splits[1], (TOKENS, D), 1.0, 6.0, ((0, 8), (1, 32)))
    up_tiles = gaussian(splits[2], (N_MP * MAXB, BLK, BLK), (D // 4) ** -0.5, 0.1875, ((0, 32),))
    up_rows = draw_up_rows(jax.random.fold_in(splits[10], 71), 0)
    up_columns = draw_up_columns(jax.random.fold_in(splits[10], 71), 0)
    up_counts = draw_up_counts(jax.random.fold_in(splits[10], 71), 0)
    down_tiles = gaussian(splits[6], (N_MP * MAXB, BLK, BLK), (FF // 4) ** -0.5, 0.09375, ((0, 32),))
    down_rows = draw_down_rows(jax.random.fold_in(splits[10], 71), 0)
    down_columns = draw_down_columns(jax.random.fold_in(splits[10], 71), 0)
    down_counts = draw_down_counts(jax.random.fold_in(splits[10], 71), 0)
    return dict(tokens=tokens, cotangent=cotangent, up_tiles=up_tiles, up_rows=up_rows, up_columns=up_columns, up_counts=up_counts, down_tiles=down_tiles, down_rows=down_rows, down_columns=down_columns, down_counts=down_counts)


def gelu_value(values):
    return 0.5 * values * (1.0 + jax.scipy.special.erf(values * 0.7071067811865476))

def gelu_slope(values):
    return 0.5 * (1.0 + jax.scipy.special.erf(values * 0.7071067811865476)) + values * jnp.exp(-0.5 * values * values) * 0.3989422804014327

def pick_table(labels, count):
    return (labels[:, None] == jnp.arange(count, dtype=jnp.int32)[None, :]).astype(jnp.float32)

def reference(tokens, cotangent, up_tiles, up_rows, up_columns, up_counts, down_tiles, down_rows, down_columns, down_counts):
    highest = lax.Precision.HIGHEST
    tok_rows = tokens.shape[0]
    grad_scale = 1.0 / math.sqrt(TOKENS)
    token_blocks = tokens.reshape(tok_rows, DB, BLK)
    cot_blocks = cotangent.reshape(tok_rows, DB, BLK)
    slot_ids = jnp.arange(MAXB, dtype=jnp.int32)
    places = jnp.arange(N_MP, dtype=jnp.int32)
    up_set = (up_tiles.reshape(N_MP, MAXB, BLK, BLK), up_rows.reshape(N_MP, MAXB).astype(jnp.int32), up_columns.reshape(N_MP, MAXB).astype(jnp.int32), up_counts.astype(jnp.int32), places)
    down_set = (down_tiles.reshape(N_MP, MAXB, BLK, BLK), down_rows.reshape(N_MP, MAXB).astype(jnp.int32), down_columns.reshape(N_MP, MAXB).astype(jnp.int32), down_counts.astype(jnp.int32), places)

    def forward_device(item):
        tiles, rows, columns, count, place = item
        live = (slot_ids < count).astype(jnp.float32)
        gathered = token_blocks[:, rows].astype(jnp.float32)
        terms = jnp.einsum('tsk,skn->tsn', gathered, tiles.astype(jnp.float32), precision=highest) * live[None, :, None]
        table = pick_table(columns - place * HB, HB)
        return jnp.einsum('tsn,sc->tcn', terms, table, precision=highest).reshape(tok_rows, HB * BLK)
    pre_all = lax.map(forward_device, up_set)
    active_all = gelu_value(pre_all).astype(jnp.bfloat16)

    def output_step(total, item):
        active_part, tiles, rows, columns, count, place = item
        live = (slot_ids < count).astype(jnp.float32)
        gathered = active_part.reshape(tok_rows, HB, BLK)[:, rows - place * HB].astype(jnp.float32)
        terms = jnp.einsum('tsk,skn->tsn', gathered, tiles.astype(jnp.float32), precision=highest) * live[None, :, None]
        partial_out = jnp.einsum('tsn,sd->tdn', terms, pick_table(columns, DB), precision=highest).reshape(tok_rows, D)
        rounded = lax.optimization_barrier(partial_out.astype(jnp.bfloat16))
        return (total + rounded.astype(jnp.float32), None)
    out_total, _ = lax.scan(output_step, jnp.zeros((tok_rows, D), jnp.float32), (active_all,) + down_set)
    mixed = out_total.astype(jnp.bfloat16)

    def backward_device(item):
        pre_part, active_part, tiles, rows, columns, count, place = item
        live = (slot_ids < count).astype(jnp.float32)
        local_rows = rows - place * HB
        cot_gathered = cot_blocks[:, columns].astype(jnp.float32)
        back_terms = jnp.einsum('tsn,skn->tsk', cot_gathered, tiles.astype(jnp.float32), precision=highest) * live[None, :, None]
        back_hidden = jnp.einsum('tsk,sc->tck', back_terms, pick_table(local_rows, HB), precision=highest).reshape(tok_rows, HB * BLK)
        slope = (back_hidden * gelu_slope(pre_part)).astype(jnp.bfloat16)
        act_gathered = active_part.reshape(tok_rows, HB, BLK)[:, local_rows].astype(jnp.float32)
        down_grad = jnp.einsum('tsk,tsn->skn', act_gathered, cot_gathered, precision=highest) * live[:, None, None] * grad_scale
        return (slope, down_grad)
    slope_all, down_grads = lax.map(backward_device, (pre_all, active_all) + down_set)

    def input_step(total, item):
        slope_part, tiles, rows, columns, count, place = item
        live = (slot_ids < count).astype(jnp.float32)
        slope_gathered = slope_part.reshape(tok_rows, HB, BLK)[:, columns - place * HB].astype(jnp.float32)
        terms = jnp.einsum('tsn,skn->tsk', slope_gathered, tiles.astype(jnp.float32), precision=highest) * live[None, :, None]
        partial_back = jnp.einsum('tsk,sd->tdk', terms, pick_table(rows, DB), precision=highest).reshape(tok_rows, D)
        rounded = lax.optimization_barrier(partial_back.astype(jnp.bfloat16))
        token_gathered = token_blocks[:, rows].astype(jnp.float32)
        up_grad = jnp.einsum('tsk,tsn->skn', token_gathered, slope_gathered, precision=highest) * live[:, None, None] * grad_scale
        return (total + rounded.astype(jnp.float32), up_grad)
    back_total, up_grads = lax.scan(input_step, jnp.zeros((tok_rows, D), jnp.float32), (slope_all,) + up_set)
    token_grads = back_total.astype(jnp.bfloat16)
    return (mixed, token_grads, up_grads.reshape(N_MP * MAXB, BLK, BLK), down_grads.reshape(N_MP * MAXB, BLK, BLK))
```

```python
import functools
import math

import jax
import jax.numpy as jnp
from jax import lax
from jax.experimental import pallas as pl
from jax.experimental.pallas import tpu as pltpu
from jax.sharding import PartitionSpec as P

BLK = 256
HALF = 128
SLOTS = 12
ROWS = 768
MY_ROWS = 384
GROUPS = 3
PER = SLOTS // GROUPS
SLICE = 32
MESH = pl.DeviceIdType.MESH
BF = jnp.bfloat16
F32 = jnp.float32


def pack_pattern(rows, hidden, place, count):
    slot = jnp.arange(SLOTS, dtype=jnp.int32)
    local_hidden = hidden - place * 2
    pair = jnp.where(slot < count, local_hidden * 16 + rows, -1)
    match = pair[None, :] == jnp.arange(32, dtype=jnp.int32)[:, None]
    table = jnp.sum(jnp.where(match, slot[None, :] + 1, 0), axis=1)
    return table, local_hidden


def kernel(
    tok_in, cot_in, up_in, dn_in, meta_in,
    mixed_out, tg_out, ug_out, dg_out,
    acts_in, up_own, dn_own, up_other, dn_other, meta_v, meta_s, pre, bh, act, slope,
    pbuf, sbuf, rbuf, frecv,
    gd, gdr, gds, gdr2, gu, gur, gus, gur2,
    local_sem, swap_s, swap_r, z_s, z_r, sib_s, sib_r, w_s, w_r,
    rsib_s, rsib_r, ring_s, ring_r, fin_s, fin_r, g_s, g_r,
):
    d = lax.axis_index("dp")
    m = lax.axis_index("mp")
    y = lax.rem(d, 4)
    x_hi = d // 4
    z = m // 4
    x = lax.rem(m // 2, 2)
    c = lax.rem(m, 2)
    other_x = 1 - x
    other_c = 1 - c

    def place(hi, yy, zz, lo, cc):
        return (hi * 4 + yy, zz * 4 + lo * 2 + cc)

    z_next = place(x_hi, y, lax.rem(z + 1, 8), x, c)
    z_prev = place(x_hi, y, lax.rem(z + 7, 8), x, c)
    sibling = place(x_hi, y, z, x, other_c)
    partner = place(x_hi, y, z, other_x, c)
    flip_hi = 1 - x_hi
    x_up = place(lax.rem(x_hi + x, 2), y, z, other_x, c)
    x_down = place(lax.rem(x_hi + other_x, 2), y, z, other_x, c)
    x_peers = [partner, place(flip_hi, y, z, x, c), place(flip_hi, y, z, other_x, c)]
    peer_hi = [x_hi, flip_hi, flip_hi]
    peer_p = [1, 0, 1]
    y_peers = [place(x_hi, lax.rem(y + j, 4), z, x, c) for j in (1, 2, 3)]

    started = []

    def send(src, dst, s, r, dev):
        copy = pltpu.make_async_remote_copy(
            src_ref=src, dst_ref=dst, send_sem=s, recv_sem=r, device_id=dev, device_id_type=MESH
        )
        copy.start()
        started.append(copy)

    def arrived(ref, s, r):
        pltpu.make_async_remote_copy(
            src_ref=ref, dst_ref=ref, send_sem=s, recv_sem=r, device_id=sibling, device_id_type=MESH
        ).wait_recv()

    my_rows = pl.ds(pl.multiple_of(x * MY_ROWS, MY_ROWS), MY_ROWS)
    their_rows = pl.ds(pl.multiple_of(other_x * MY_ROWS, MY_ROWS), MY_ROWS)
    ins = [tok_in, cot_in]
    tiles = [[up_own, up_other], [dn_own, dn_other]]
    locals_ = []
    for a in range(2):
        locals_.append(
            pltpu.make_async_copy(ins[a].at[my_rows], acts_in.at[a, 0, c, x], local_sem.at[a])
        )
    for k, ref in enumerate((up_in, dn_in)):
        locals_.append(
            pltpu.make_async_copy(ref, tiles[k][0], local_sem.at[2 + k])
        )
    locals_.append(pltpu.make_async_copy(meta_in, meta_s.at[0], local_sem.at[4]))
    for copy in locals_:
        copy.start()

    barrier = pltpu.get_barrier_semaphore()
    peers = [z_next, z_prev, sibling] + x_peers + y_peers
    for dev in peers:
        pl.semaphore_signal(barrier, inc=1, device_id=dev, device_id_type=MESH)
    pl.semaphore_wait(barrier, len(peers))

    for a in range(2):
        send(ins[a].at[their_rows], acts_in.at[a, 0, c, x], swap_s.at[a], swap_r.at[a], partner)
    send(meta_in, meta_v, swap_s.at[2], swap_r.at[2], partner)

    def z_send(a, direction, index, src, dst):
        send(src, dst, z_s.at[a, direction, index], z_r.at[a, direction, index],
             z_prev if direction else z_next)

    def z_wait(a, direction, index, ref):
        arrived(ref, z_s.at[a, direction, index], z_r.at[a, direction, index])

    def sib_send(a, r):
        ref = acts_in.at[a, r, c]
        send(ref, ref, sib_s.at[a, r], sib_r.at[a, r], sibling)

    def sib_wait(a, r):
        arrived(acts_in.at[a, r, other_c], sib_s.at[a, r], sib_r.at[a, r])

    for a in range(2):
        locals_[a].wait()
        for direction, r in ((0, 1), (1, 7)):
            z_send(a, direction, 0, acts_in.at[a, 0, c, x], acts_in.at[a, r, c, x])
    for k in range(2):
        locals_[2 + k].wait()
        for half, dev in ((0, x_up), (1, x_down)):
            send(
                tiles[k][0].at[pl.ds(half * 6, 6)], tiles[k][1].at[pl.ds(half * 6, 6)],
                w_s.at[k, half], w_r.at[k, half], dev,
            )
    for a in range(2):
        arrived(acts_in.at[a, 0, c, other_x], swap_s.at[a], swap_r.at[a])
        for direction, r in ((0, 1), (1, 7)):
            z_send(a, direction, 1, acts_in.at[a, 0, c, other_x], acts_in.at[a, r, c, other_x])
        sib_send(a, 0)
    locals_[4].wait()
    arrived(meta_v, swap_s.at[2], swap_r.at[2])
    to_smem = pltpu.make_async_copy(meta_v, meta_s.at[1], local_sem.at[5])
    to_smem.start()

    def tile(kind, p, h, b):
        found = meta_s[p, kind, h * 16 + b]
        value = tiles[kind][p][jnp.maximum(found - 1, 0)]
        return jnp.where(found > 0, value, jnp.zeros_like(value))

    sums = [pre, bh]

    def accumulate(a, p, r, first):
        left = jnp.concatenate(
            [acts_in[a, r, 0, 0], acts_in[a, r, 1, 0], acts_in[a, r, 0, 1], acts_in[a, r, 1, 1]], axis=1
        )
        b = 2 * lax.rem(z + 8 - r, 8)
        for h in range(2):
            w0, w1 = tile(a, p, h, b), tile(a, p, h, b + 1)
            if a == 0:
                out = jnp.dot(left, jnp.concatenate([w0, w1], axis=0), preferred_element_type=F32)
            else:
                out = lax.dot_general(
                    left, jnp.concatenate([w0, w1], axis=1), (((1,), (1,)), ((), ())),
                    preferred_element_type=F32,
                )
            if first:
                sums[a][p * 2 + h] = out
            else:
                sums[a][p * 2 + h] += out

    for k in (1, 2, 3):
        for a in range(2):
            for direction, r in ((0, k), (1, 8 - k)):
                if k == 1:
                    z_wait(a, direction, 0, acts_in.at[a, r, c, x])
                    z_wait(a, direction, 1, acts_in.at[a, r, c, other_x])
                else:
                    z_wait(a, direction, k, acts_in.at[a, r, c])
                if k < 3:
                    z_send(a, direction, k + 1, acts_in.at[a, r, c],
                           acts_in.at[a, r + 1 - 2 * direction, c])
                else:
                    z_send(a, direction, 4, acts_in.at[a, r, c, direction],
                           acts_in.at[a, 4, c, direction])
                sib_send(a, r)
        for a in range(2):
            for r in ((0,) if k == 1 else (k - 1, 9 - k)):
                sib_wait(a, r)
                accumulate(a, 0, r, k == 1)
    for a in range(2):
        for direction in range(2):
            z_wait(a, direction, 4, acts_in.at[a, 4, c, direction])
        sib_send(a, 4)
    to_smem.wait()
    for a in range(2):
        for half in range(2):
            arrived(tiles[a][1].at[pl.ds(half * 6, 6)], w_s.at[a, half], w_r.at[a, half])
        for r in (3, 5, 4):
            sib_wait(a, r)
            accumulate(a, 0, r, False)
        accumulate(a, 1, 0, True)

        def rest(r, carry, a=a):
            accumulate(a, 1, r, False)
            return carry

        lax.fori_loop(1, 8, rest, 0)
        if a == 0:

            def gelu_step(i, carry):
                h = i // 6
                rows = pl.ds(pl.multiple_of(lax.rem(i, 6) * 64, 64), 64)
                v = pre[h, rows]
                cdf = 0.5 * (1.0 + lax.erf(v * 0.7071067811865476))
                act[h, rows] = (v * cdf).astype(BF)
                pre[h, rows] = cdf + v * jnp.exp(-0.5 * v * v) * 0.3989422804014327
                return carry

            lax.fori_loop(0, 24, gelu_step, 0)

    def slope_step(i, carry):
        h = i // 6
        rows = pl.ds(pl.multiple_of(lax.rem(i, 6) * 64, 64), 64)
        slope[h, rows] = (bh[h, rows] * pre[h, rows]).astype(BF)
        return carry

    lax.fori_loop(0, 24, slope_step, 0)

    lefts = [act, slope]

    def partial(o, q):
        left = jnp.concatenate([lefts[o][h] for h in range(4)], axis=1)
        b = 2 * lax.rem(z + q, 8)
        kind = 1 - o
        for xx in range(2):
            ws = [tile(kind, h // 2, h % 2, b + xx) for h in range(4)]
            if o == 0:
                out = jnp.dot(left, jnp.concatenate(ws, axis=0), preferred_element_type=F32)
            else:
                out = lax.dot_general(
                    left, jnp.concatenate(ws, axis=1), (((1,), (1,)), ((), ())),
                    preferred_element_type=F32,
                )
            out = out.astype(BF)
            for half in range(2):
                pbuf[o, q, half, xx] = out[:, half * HALF:(half + 1) * HALF]
        send(pbuf.at[o, q, other_c], sbuf.at[o, q], rsib_s.at[o, q], rsib_r.at[o, q], sibling)

    def add_sibling(o, q, extra):
        arrived(sbuf.at[o, q], rsib_s.at[o, q], rsib_r.at[o, q])
        for xx in range(2):
            total = pbuf[o, q, c, xx].astype(F32) + sbuf[o, q, xx].astype(F32)
            for more in extra[xx]:
                total += more().astype(F32)
            pbuf[o, q, c, xx] = total.astype(BF)

    def ring_send(o, direction, step, src, dst):
        send(src, dst, ring_s.at[o, direction, step], ring_r.at[o, direction, step],
             z_prev if direction else z_next)

    def ring_wait(o, direction, step, ref):
        arrived(ref, ring_s.at[o, direction, step], ring_r.at[o, direction, step])

    scale = 1.0 / math.sqrt(ROWS * 8)

    def grad_product(kind, p, i):
        if kind == 0:
            block, h = meta_s[p, 2, i], meta_s[p, 3, i]
        else:
            block, h = meta_s[p, 5, i], meta_s[p, 4, i]
        r = lax.rem(z + 8 - block // 2, 8)
        xx = lax.rem(block, 2)
        wide = jnp.concatenate([acts_in[kind, r, 0, xx], acts_in[kind, r, 1, xx]], axis=1)
        hidden = lefts[1 - kind][p * 2 + h]
        a, b = (wide, hidden) if kind == 0 else (hidden, wide)
        out = lax.dot_general(a, b, (((0,), (0,)), ((), ())), preferred_element_type=F32)
        live = jnp.where(i < meta_s[p, 6, kind], scale, 0.0)
        return (out * live).astype(BF)

    def down_group(g):
        def one(t, carry):
            p, i = t // PER, lax.rem(t, PER)
            out = grad_product(1, p, g * PER + i)
            for part in range(8):
                gd[g, part % 4, part // 4, p, i] = out[part * SLICE:(part + 1) * SLICE]
            return carry

        lax.fori_loop(0, 2 * PER, one, 0)
        for j in range(3):
            send(gd.at[g, lax.rem(y + j + 1, 4)], gdr.at[g, j],
                 g_s.at[0, g, j], g_r.at[0, g, j], y_peers[j])

    def up_group(g):
        def one(t, carry):
            p, i = t // PER, lax.rem(t, PER)
            out = grad_product(0, p, g * PER + i)
            for part in range(8):
                gu[g, part // 4, p, part % 4, i] = out[part * SLICE:(part + 1) * SLICE]
            return carry

        lax.fori_loop(0, 2 * PER, one, 0)
        for j in range(3):
            send(gu.at[g, peer_hi[j], peer_p[j]], gur.at[g, j],
                 g_s.at[1, g, j], g_r.at[1, g, j], x_peers[j])

    def down_second(g):
        for j in range(3):
            arrived(gdr.at[g, j], g_s.at[0, g, j], g_r.at[0, g, j])
        for hi in range(2):
            for p in range(2):
                total = gd[g, y, hi, p].astype(F32)
                for j in range(3):
                    total += gdr[g, j, hi, p].astype(F32)
                gds[g, hi, p] = total.astype(BF)
        for j in range(3):
            send(gds.at[g, peer_hi[j], peer_p[j]], gdr2.at[g, j],
                 g_s.at[2, g, j], g_r.at[2, g, j], x_peers[j])

    def up_second(g):
        for j in range(3):
            arrived(gur.at[g, j], g_s.at[1, g, j], g_r.at[1, g, j])
        for yy in range(4):
            total = gu[g, x_hi, 0, yy].astype(F32)
            for j in range(3):
                total += gur[g, j, yy].astype(F32)
            gus[g, yy] = total.astype(BF)
        for j in range(3):
            send(gus.at[g, lax.rem(y + j + 1, 4)], gur2.at[g, j],
                 g_s.at[3, g, j], g_r.at[3, g, j], y_peers[j])

    def down_last(g):
        for j in range(3):
            arrived(gdr2.at[g, j], g_s.at[2, g, j], g_r.at[2, g, j])
        total = gds[g, x_hi, 0].astype(F32)
        for j in range(3):
            total += gdr2[g, j].astype(F32)
        dg_out[g * PER:(g + 1) * PER] = total

    def up_last(g):
        for j in range(3):
            arrived(gur2.at[g, j], g_s.at[3, g, j], g_r.at[3, g, j])
        total = gus[g, y].astype(F32)
        for j in range(3):
            total += gur2[g, j].astype(F32)
        ug_out[g * PER:(g + 1) * PER] = total

    for o in range(2):
        partial(o, 4)
    down_group(0)
    up_group(0)
    for o in range(2):
        add_sibling(o, 4, [[], []])
        for direction in range(2):
            ring_send(o, direction, 0, pbuf.at[o, 4, c, direction], rbuf.at[o, direction, 0, direction])
        partial(o, 3)
        partial(o, 5)
    down_group(1)
    up_group(1)
    for step in (1, 2, 3):
        for o in range(2):
            for direction in range(2):
                q = 4 + step if direction else 4 - step
                came = rbuf.at[o, direction, step - 1]
                if step == 1:
                    ring_wait(o, direction, 0, came.at[direction])
                    extra = [[], []]
                    extra[direction] = [lambda came=came, xx=direction: came[xx]]
                else:
                    ring_wait(o, direction, step - 1, came)
                    extra = [[lambda came=came, xx=xx: came[xx]] for xx in range(2)]
                add_sibling(o, q, extra)
                ring_send(o, direction, step, pbuf.at[o, q, c], rbuf.at[o, direction, step])
            if step < 3:
                partial(o, 3 - step)
                partial(o, 5 + step)
            else:
                partial(o, 0)
        if step == 1:
            down_group(2)
            up_group(2)
    for g in range(GROUPS):
        down_second(g)
        up_second(g)
    outs = [mixed_out, tg_out]
    for o in range(2):
        for direction in range(2):
            ring_wait(o, direction, 3, rbuf.at[o, direction, 3])
        add_sibling(
            o, 0,
            [[lambda xx=xx, e=e: rbuf[o, e, 3, xx] for e in range(2)] for xx in range(2)],
        )
        send(pbuf.at[o, 0, c, other_x], frecv.at[o], fin_s.at[o], fin_r.at[o], partner)
        outs[o][my_rows] = pbuf[o, 0, c, x]
    for g in range(GROUPS):
        down_last(g)
        up_last(g)
    for o in range(2):
        arrived(frecv.at[o], fin_s.at[o], fin_r.at[o])
        outs[o][their_rows] = frecv[o]
    for copy in started:
        copy.wait_send()


def local(
    tokens, cotangent, up_tiles, up_rows, up_columns, up_counts,
    down_tiles, down_rows, down_columns, down_counts,
):
    place = lax.axis_index("mp")
    up_table, up_hidden = pack_pattern(up_rows, up_columns, place, up_counts[0])
    down_table, down_hidden = pack_pattern(down_columns, down_rows, place, down_counts[0])
    counts = jnp.concatenate([up_counts, down_counts])
    meta = jnp.stack(
        [
            jnp.pad(v, (0, 128 - v.shape[0]))
            for v in (up_table, down_table, up_rows, up_hidden, down_hidden, down_columns, counts, counts)
        ]
    )
    dma = pltpu.SemaphoreType.DMA
    vm = pltpu.VMEM
    any_space = pl.BlockSpec(memory_space=pl.ANY)
    in_vmem = pl.BlockSpec(memory_space=pltpu.VMEM)
    return tuple(
        pl.pallas_call(
            kernel,
            out_shape=(
                jax.ShapeDtypeStruct((ROWS, HALF), BF),
                jax.ShapeDtypeStruct((ROWS, HALF), BF),
                jax.ShapeDtypeStruct((SLOTS, SLICE, BLK), F32),
                jax.ShapeDtypeStruct((SLOTS, SLICE, BLK), F32),
            ),
            in_specs=[any_space] * 4 + [in_vmem],
            out_specs=(in_vmem,) * 4,
            scratch_shapes=[
                vm((2, 8, 2, 2, MY_ROWS, HALF), BF),
                vm((SLOTS, BLK, BLK), BF), vm((SLOTS, BLK, BLK), BF),
                vm((SLOTS, BLK, BLK), BF), vm((SLOTS, BLK, BLK), BF),
                vm((8, 128), jnp.int32),
                pltpu.SMEM((2, 8, 128), jnp.int32),
                vm((4, MY_ROWS, BLK), F32),
                vm((4, MY_ROWS, BLK), F32),
                vm((4, MY_ROWS, BLK), BF),
                vm((4, MY_ROWS, BLK), BF),
                vm((2, 8, 2, 2, MY_ROWS, HALF), BF),
                vm((2, 8, 2, MY_ROWS, HALF), BF),
                vm((2, 2, 4, 2, MY_ROWS, HALF), BF),
                vm((2, MY_ROWS, HALF), BF),
                vm((GROUPS, 4, 2, 2, PER, SLICE, BLK), BF),
                vm((GROUPS, 3, 2, 2, PER, SLICE, BLK), BF),
                vm((GROUPS, 2, 2, PER, SLICE, BLK), BF),
                vm((GROUPS, 3, PER, SLICE, BLK), BF),
                vm((GROUPS, 2, 2, 4, PER, SLICE, BLK), BF),
                vm((GROUPS, 3, 4, PER, SLICE, BLK), BF),
                vm((GROUPS, 4, PER, SLICE, BLK), BF),
                vm((GROUPS, 3, PER, SLICE, BLK), BF),
                dma((6,)),
                dma((3,)), dma((3,)),
                dma((2, 2, 5)), dma((2, 2, 5)),
                dma((2, 8)), dma((2, 8)),
                dma((2, 2)), dma((2, 2)),
                dma((2, 8)), dma((2, 8)),
                dma((2, 2, 4)), dma((2, 2, 4)),
                dma((2,)), dma((2,)),
                dma((4, GROUPS, 3)), dma((4, GROUPS, 3)),
            ],
            compiler_params=pltpu.CompilerParams(
                collective_id=0, has_side_effects=True, vmem_limit_bytes=58 << 20
            ),
            name="sparse_feed_forward",
        )(tokens, cotangent, up_tiles, down_tiles, meta)
    )


def solution(mesh):
    return jax.shard_map(
        local,
        mesh=mesh,
        in_specs=(
            P("dp", "mp"),
            P("dp", "mp"),
            P("mp", None, None),
            P("mp"),
            P("mp"),
            P("mp"),
            P("mp", None, None),
            P("mp"),
            P("mp"),
            P("mp"),
        ),
        out_specs=(P("dp", "mp"), P("dp", "mp"), P("mp", "dp", None), P("mp", "dp", None)),
        check_vma=False,
    )
```

```python
import functools
import math

import jax
import jax.numpy as jnp
from jax import lax
from jax.experimental import pallas as pl
from jax.experimental.pallas import tpu as pltpu
from jax.sharding import PartitionSpec as P

BLK = 256
HALF = 128
SLOTS = 12
ROWS = 768
MY_ROWS = 384
GROUPS = 3
PER = SLOTS // GROUPS
SLICE = 32
MESH = pl.DeviceIdType.MESH
BF = jnp.bfloat16
F32 = jnp.float32


def pack_pattern(up_rows, up_columns, up_counts, down_rows, down_columns, down_counts):
    lane = lax.broadcasted_iota(jnp.int32, (8, 128), 1)
    row = lax.broadcasted_iota(jnp.int32, (8, 128), 0)
    ups, downs = up_counts[0], down_counts[0]
    packed = jnp.where((row == 6) & (lane == 0), ups, 0)
    packed = jnp.where((row == 6) & (lane == 1), downs, packed)
    for s in range(SLOTS):
        up_row, up_hidden = up_rows[s], up_columns[s] & 1
        down_hidden, down_column = down_rows[s] & 1, down_columns[s]
        up_pair = jnp.where(s < ups, up_hidden * 16 + up_row, -1)
        down_pair = jnp.where(s < downs, down_hidden * 16 + down_column, -1)
        found = ((row == 0) & (lane == up_pair)) | ((row == 1) & (lane == down_pair))
        packed = jnp.where(found, s + 1, packed)
        for at, value in ((2, up_row), (3, up_hidden), (4, down_hidden), (5, down_column)):
            packed = jnp.where((row == at) & (lane == s), value, packed)
    return packed


def kernel(
    tok_in, cot_in, up_in, dn_in, up_rows, up_columns, up_counts, down_rows, down_columns, down_counts,
    mixed_out, tg_out, ug_out, dg_out,
    acts_in, up_own, dn_own, up_other, dn_other, meta_own, meta_v, meta_s, pre, bh, act, slope, tok_t, act_t,
    pbuf, sbuf, rbuf, frecv,
    gd, gda, gdr, gds, gdr2, gu, gua, gur, gus, gur2,
    local_sem, swap_s, swap_r, z_s, z_r, sib_s, sib_r, w_s, w_r,
    rsib_s, rsib_r, ring_s, ring_r, fin_s, fin_r, g_s, g_r,
):
    d = lax.axis_index("dp")
    m = lax.axis_index("mp")
    y = lax.rem(d, 4)
    x_hi = d // 4
    z = m // 4
    x = lax.rem(m // 2, 2)
    c = lax.rem(m, 2)
    other_x = 1 - x
    other_c = 1 - c

    def place(hi, yy, zz, lo, cc):
        return (hi * 4 + yy, zz * 4 + lo * 2 + cc)

    z_next = place(x_hi, y, lax.rem(z + 1, 8), x, c)
    z_prev = place(x_hi, y, lax.rem(z + 7, 8), x, c)
    sibling = place(x_hi, y, z, x, other_c)
    partner = place(x_hi, y, z, other_x, c)
    flip_hi = 1 - x_hi
    x_up = place(lax.rem(x_hi + x, 2), y, z, other_x, c)
    x_down = place(lax.rem(x_hi + other_x, 2), y, z, other_x, c)
    x_peers = [partner, place(flip_hi, y, z, x, c), place(flip_hi, y, z, other_x, c)]
    peer_hi = [x_hi, flip_hi, flip_hi]
    peer_p = [1, 0, 1]
    y_peers = [place(x_hi, lax.rem(y + j, 4), z, x, c) for j in (1, 2, 3)]

    barrier = pltpu.get_barrier_semaphore()
    peers = [z_next, z_prev, sibling] + x_peers + y_peers
    for dev in peers:
        pl.semaphore_signal(barrier, inc=1, device_id=dev, device_id_type=MESH)

    started = []

    def send(src, dst, s, r, dev):
        copy = pltpu.make_async_remote_copy(
            src_ref=src, dst_ref=dst, send_sem=s, recv_sem=r, device_id=dev, device_id_type=MESH
        )
        copy.start()
        started.append(copy)

    def arrived(ref, s, r):
        pltpu.make_async_remote_copy(
            src_ref=ref, dst_ref=ref, send_sem=s, recv_sem=r, device_id=sibling, device_id_type=MESH
        ).wait_recv()

    my_rows = pl.ds(pl.multiple_of(x * MY_ROWS, MY_ROWS), MY_ROWS)
    their_rows = pl.ds(pl.multiple_of(other_x * MY_ROWS, MY_ROWS), MY_ROWS)
    ins = [tok_in, cot_in]
    tiles = [[up_own, up_other], [dn_own, dn_other]]
    locals_ = []
    for a in range(2):
        locals_.append(
            pltpu.make_async_copy(ins[a].at[my_rows], acts_in.at[a, 0, c, x], local_sem.at[a])
        )
    for k, ref in enumerate((up_in, dn_in)):
        locals_.append(
            pltpu.make_async_copy(ref, tiles[k][0], local_sem.at[2 + k])
        )
    for copy in locals_:
        copy.start()
    meta_own[...] = pack_pattern(up_rows, up_columns, up_counts, down_rows, down_columns, down_counts)
    locals_.append(pltpu.make_async_copy(meta_own, meta_s.at[0], local_sem.at[4]))
    locals_[4].start()

    pl.semaphore_wait(barrier, len(peers))

    for a in range(2):
        send(ins[a].at[their_rows], acts_in.at[a, 0, c, x], swap_s.at[a], swap_r.at[a], partner)
    send(meta_own, meta_v, swap_s.at[2], swap_r.at[2], partner)

    def z_send(a, direction, step, block, src, dst):
        send(src, dst, z_s.at[a, direction, step, block], z_r.at[a, direction, step, block],
             z_prev if direction else z_next)

    def z_wait(a, direction, step, block, ref):
        arrived(ref, z_s.at[a, direction, step, block], z_r.at[a, direction, step, block])

    def sib_send(a, r):
        ref = acts_in.at[a, r, c]
        send(ref, ref, sib_s.at[a, r], sib_r.at[a, r], sibling)

    def sib_wait(a, r):
        arrived(acts_in.at[a, r, other_c], sib_s.at[a, r], sib_r.at[a, r])

    def quarter(i):
        return pl.ds(3 * lax.rem(y + i, 4), 3)

    def send_own(a):
        locals_[a].wait()
        for direction, r in ((0, 1), (1, 7)):
            z_send(a, direction, 0, x, acts_in.at[a, 0, c, x], acts_in.at[a, r, c, x])

    def swap_done(a):
        arrived(acts_in.at[a, 0, c, other_x], swap_s.at[a], swap_r.at[a])
        sib_send(a, 0)

    def send_swapped(a):
        for direction, r in ((0, 1), (1, 7)):
            z_send(a, direction, 0, other_x, acts_in.at[a, 0, c, other_x], acts_in.at[a, r, c, other_x])

    send_own(0)
    for k in range(2):
        locals_[2 + k].wait()
        for i, dev in ((0, x_up), (1, x_down)):
            send(tiles[k][0].at[quarter(i)], tiles[k][1].at[quarter(i)], w_s.at[k, i], w_r.at[k, i], dev)
    swap_done(0)
    send_swapped(0)
    send_own(1)
    locals_[4].wait()
    arrived(meta_v, swap_s.at[2], swap_r.at[2])
    to_smem = pltpu.make_async_copy(meta_v, meta_s.at[1], local_sem.at[5])
    to_smem.start()
    swap_done(1)

    def tile(kind, p, h, b):
        found = meta_s[p, kind, h * 16 + b]
        value = tiles[kind][p][jnp.maximum(found - 1, 0)]
        return jnp.where(found > 0, value, jnp.zeros_like(value))

    def pass_weights(k):
        for i, j, dev in ((0, 3, y_peers[0]), (1, 2, y_peers[2])):
            ref = tiles[k][1].at[quarter(i)]
            arrived(ref, w_s.at[k, i], w_r.at[k, i])
            send(ref, ref, w_s.at[k, j], w_r.at[k, j], dev)

    def rest_of_weights(k):
        for j in (2, 3):
            arrived(tiles[k][1].at[quarter(j)], w_s.at[k, j], w_r.at[k, j])

    sums = [pre, bh]

    def accumulate(a, p, r, first):
        left = jnp.concatenate(
            [acts_in[a, r, 0, 0], acts_in[a, r, 1, 0], acts_in[a, r, 0, 1], acts_in[a, r, 1, 1]], axis=1
        )
        if a == 0 and p == 0:
            for xx in range(2):
                tok_t[r, xx] = left[:, xx * BLK:(xx + 1) * BLK].T
        b = 2 * lax.rem(z + 8 - r, 8)
        for h in range(2):
            w0, w1 = tile(a, p, h, b), tile(a, p, h, b + 1)
            if a == 0:
                out = jnp.dot(left, jnp.concatenate([w0, w1], axis=0), preferred_element_type=F32)
            else:
                out = lax.dot_general(
                    left, jnp.concatenate([w0, w1], axis=1), (((1,), (1,)), ((), ())),
                    preferred_element_type=F32,
                )
            if first:
                sums[a][p * 2 + h] = out
            else:
                sums[a][p * 2 + h] += out

    def forward(a, k):
        for block in (x, other_x):
            for direction, r in ((0, k), (1, 8 - k)):
                z_wait(a, direction, k - 1, block, acts_in.at[a, r, c, block])
                if k < 3:
                    z_send(a, direction, k, block, acts_in.at[a, r, c, block],
                           acts_in.at[a, r + 1 - 2 * direction, c, block])
        for direction, r in ((0, k), (1, 8 - k)):
            if k == 3:
                z_send(a, direction, 3, direction, acts_in.at[a, r, c, direction],
                       acts_in.at[a, 4, c, direction])
            sib_send(a, r)

    def last_unit(a):
        for direction in range(2):
            z_wait(a, direction, 3, direction, acts_in.at[a, 4, c, direction])
        sib_send(a, 4)

    def own_products(a, units):
        for r in units:
            sib_wait(a, r)
            accumulate(a, 0, r, r == 0)

    def other_products(a):
        accumulate(a, 1, 0, True)

        def rest(r, carry):
            accumulate(a, 1, r, False)
            return carry

        lax.fori_loop(1, 8, rest, 0)

    def gelu_step(i, carry):
        h = i // 6
        rows = pl.ds(pl.multiple_of(lax.rem(i, 6) * 64, 64), 64)
        v = pre[h, rows]
        cdf = 0.5 * (1.0 + lax.erf(v * 0.7071067811865476))
        act[h, rows] = (v * cdf).astype(BF)
        pre[h, rows] = cdf + v * jnp.exp(-0.5 * v * v) * 0.3989422804014327
        return carry

    def slope_step(i, carry):
        h = i // 6
        rows = pl.ds(pl.multiple_of(lax.rem(i, 6) * 64, 64), 64)
        slope[h, rows] = (bh[h, rows] * pre[h, rows]).astype(BF)
        return carry

    lefts = [act, slope]

    def partial(o, q):
        left = jnp.concatenate([lefts[o][h] for h in range(4)], axis=1)
        b = 2 * lax.rem(z + q, 8)
        kind = 1 - o
        for xx in range(2):
            ws = [tile(kind, h // 2, h % 2, b + xx) for h in range(4)]
            if o == 0:
                out = jnp.dot(left, jnp.concatenate(ws, axis=0), preferred_element_type=F32)
            else:
                out = lax.dot_general(
                    left, jnp.concatenate(ws, axis=1), (((1,), (1,)), ((), ())),
                    preferred_element_type=F32,
                )
            out = out.astype(BF)
            for half in range(2):
                pbuf[o, q, half, xx] = out[:, half * HALF:(half + 1) * HALF]
        send(pbuf.at[o, q, other_c], sbuf.at[o, q], rsib_s.at[o, q], rsib_r.at[o, q], sibling)

    def sibling_part(o, q):
        arrived(sbuf.at[o, q], rsib_s.at[o, q], rsib_r.at[o, q])

    def add(o, q, xx, came):
        total = pbuf[o, q, c, xx].astype(F32) + sbuf[o, q, xx].astype(F32)
        for ref in came:
            total += ref[...].astype(F32)
        pbuf[o, q, c, xx] = total.astype(BF)

    def ring_send(o, direction, step, xx):
        q = 4 + step if direction else 4 - step
        send(pbuf.at[o, q, c, xx], rbuf.at[o, direction, step, xx],
             ring_s.at[o, direction, step, xx], ring_r.at[o, direction, step, xx],
             z_prev if direction else z_next)

    def ring_wait(o, direction, step, xx):
        ref = rbuf.at[o, direction, step, xx]
        arrived(ref, ring_s.at[o, direction, step, xx], ring_r.at[o, direction, step, xx])
        return ref

    def ring_first(o):
        sibling_part(o, 4)
        for direction in range(2):
            add(o, 4, direction, [])
            ring_send(o, direction, 0, direction)

    def ring_step(o, step):
        for q in (4 - step, 4 + step):
            sibling_part(o, q)
        if step == 1:
            for direction in range(2):
                add(o, 4 + step if direction else 4 - step, 1 - direction, [])
                ring_send(o, direction, step, 1 - direction)
            for direction in range(2):
                came = ring_wait(o, direction, 0, direction)
                add(o, 4 + step if direction else 4 - step, direction, [came])
                ring_send(o, direction, step, direction)
            return
        for xx in (other_x, x):
            for direction in range(2):
                came = ring_wait(o, direction, step - 1, xx)
                add(o, 4 + step if direction else 4 - step, xx, [came])
                ring_send(o, direction, step, xx)

    outs = [mixed_out, tg_out]

    def ring_last(o):
        sibling_part(o, 0)
        for xx in (other_x, x):
            add(o, 0, xx, [ring_wait(o, direction, 3, xx) for direction in range(2)])
            if xx is other_x:
                send(pbuf.at[o, 0, c, other_x], frecv.at[o], fin_s.at[o], fin_r.at[o], partner)
        outs[o][my_rows] = pbuf[o, 0, c, x]

    def gelu():
        lax.fori_loop(0, 24, gelu_step, 0)

    def slopes():
        lax.fori_loop(0, 24, slope_step, 0)

    def turn():
        for h in range(4):
            act_t[h] = act[h].T

    def fin_last(o):
        arrived(frecv.at[o], fin_s.at[o], fin_r.at[o])
        outs[o][their_rows] = frecv[o]

    scale = 1.0 / math.sqrt(ROWS * 8)

    def grad_product(kind, p, i):
        if kind == 0:
            block, h = meta_s[p, 2, i], meta_s[p, 3, i]
        else:
            block, h = meta_s[p, 5, i], meta_s[p, 4, i]
        r = lax.rem(z + 8 - block // 2, 8)
        xx = lax.rem(block, 2)
        if kind == 0:
            left, right = tok_t[r, xx], slope[p * 2 + h]
        else:
            left = act_t[p * 2 + h]
            right = jnp.concatenate([acts_in[1, r, 0, xx], acts_in[1, r, 1, xx]], axis=1)
        out = jnp.dot(left, right, preferred_element_type=F32)
        live = jnp.where(i < meta_s[p, 6, kind], scale, 0.0)
        return (out * live).astype(BF)

    y_next, y_next2, y_prev = (lax.rem(y + j, 4) for j in (1, 2, 3))
    up_hi, down_hi = lax.rem(x_hi + x, 2), lax.rem(x_hi + other_x, 2)

    def grad_send(kind, g, i, src, dst, dev):
        send(src, dst, g_s.at[kind, g, i], g_r.at[kind, g, i], dev)

    def grad_wait(kind, g, i, ref):
        arrived(ref, g_s.at[kind, g, i], g_r.at[kind, g, i])

    def down_group(g):
        def one(t, carry):
            p, i = t // PER, lax.rem(t, PER)
            out = grad_product(1, p, g * PER + i)
            for part in range(8):
                gd[g, part % 4, part // 4, p, i] = out[part * SLICE:(part + 1) * SLICE]
            return carry

        lax.fori_loop(0, 2 * PER, one, 0)
        grad_send(0, g, 0, gd.at[g, y_next2, 0], gda.at[g, 0], y_peers[0])
        grad_send(0, g, 1, gd.at[g, y_next2, 1], gda.at[g, 1], y_peers[2])

    def down_mid(g):
        for i, to, hi, dev in ((0, y_next, 0, y_peers[0]), (1, y_prev, 1, y_peers[2])):
            grad_wait(0, g, i, gda.at[g, i])
            for p in range(2):
                gd[g, to, hi, p] = (gd[g, to, hi, p].astype(F32) + gda[g, i, p].astype(F32)).astype(BF)
            grad_send(0, g, 2 + i, gd.at[g, to], gdr.at[g, i], dev)

    def up_group(g):
        def one(t, carry):
            p, i = t // PER, lax.rem(t, PER)
            out = grad_product(0, p, g * PER + i)
            for part in range(8):
                gu[g, part // 4, p, part % 4, i] = out[part * SLICE:(part + 1) * SLICE]
            return carry

        lax.fori_loop(0, 2 * PER, one, 0)
        low, high = pl.ds(0, 2), pl.ds(2, 2)
        grad_send(1, g, 0, gu.at[g, flip_hi, 0, low], gua.at[g, 0], x_up)
        grad_send(1, g, 1, gu.at[g, flip_hi, 0, high], gua.at[g, 1], x_down)

    def up_mid(g):
        for i, hi, dev in ((0, up_hi, x_up), (1, down_hi, x_down)):
            grad_wait(1, g, i, gua.at[g, i])
            for yy in range(2):
                both = gu[g, hi, 1, 2 * i + yy].astype(F32) + gua[g, i, yy].astype(F32)
                gu[g, hi, 1, 2 * i + yy] = both.astype(BF)
            grad_send(1, g, 2 + i, gu.at[g, hi, 1], gur.at[g, i], dev)

    def down_second(g):
        for i in range(2):
            grad_wait(0, g, 2 + i, gdr.at[g, i])
        for hi in range(2):
            for p in range(2):
                total = gd[g, y, hi, p].astype(F32)
                for i in range(2):
                    total += gdr[g, i, hi, p].astype(F32)
                gds[g, hi, p] = total.astype(BF)
        for j in range(3):
            grad_send(2, g, j, gds.at[g, peer_hi[j], peer_p[j]], gdr2.at[g, j], x_peers[j])

    def up_second(g):
        for i in range(2):
            grad_wait(1, g, 2 + i, gur.at[g, i])
        for yy in range(4):
            total = gu[g, x_hi, 0, yy].astype(F32)
            for i in range(2):
                total += gur[g, i, yy].astype(F32)
            gus[g, yy] = total.astype(BF)
        for j in range(3):
            grad_send(3, g, j, gus.at[g, lax.rem(y + j + 1, 4)], gur2.at[g, j], y_peers[j])

    def down_last(g):
        for j in range(3):
            grad_wait(2, g, j, gdr2.at[g, j])
        total = gds[g, x_hi, 0].astype(F32)
        for j in range(3):
            total += gdr2[g, j].astype(F32)
        dg_out[g * PER:(g + 1) * PER] = total

    def up_last(g):
        for j in range(3):
            grad_wait(3, g, j, gur2.at[g, j])
        total = gus[g, y].astype(F32)
        for j in range(3):
            total += gur2[g, j].astype(F32)
        ug_out[g * PER:(g + 1) * PER] = total

    send_swapped(1)
    forward(0, 1)
    own_products(0, (0,))
    forward(1, 1)
    pass_weights(0)
    own_products(0, (1, 7))
    forward(0, 2)
    own_products(1, (0,))
    forward(1, 2)
    own_products(0, (2, 6))
    pass_weights(1)
    forward(0, 3)
    own_products(1, (1, 7))
    to_smem.wait()
    forward(1, 3)
    last_unit(0)
    own_products(0, (3, 5))
    rest_of_weights(0)
    own_products(0, (4,))
    other_products(0)
    gelu()
    turn()
    rest_of_weights(1)
    partial(0, 4)
    partial(0, 3)
    ring_first(0)
    own_products(1, (2, 6))
    partial(0, 5)
    accumulate(1, 1, 0, True)
    accumulate(1, 1, 1, False)
    accumulate(1, 1, 7, False)
    accumulate(1, 1, 2, False)
    accumulate(1, 1, 6, False)
    last_unit(1)
    own_products(1, (3, 5))
    accumulate(1, 1, 3, False)
    accumulate(1, 1, 5, False)
    sib_wait(1, 4)
    down_group(0)
    accumulate(1, 0, 4, False)
    accumulate(1, 1, 4, False)
    slopes()
    up_group(0)
    down_group(1)
    ring_step(0, 1)
    up_group(1)
    down_group(2)
    down_mid(0)
    up_mid(0)
    up_group(2)
    partial(1, 4)
    down_mid(1)
    up_mid(1)
    ring_first(1)
    partial(0, 2)
    partial(0, 6)
    down_mid(2)
    up_mid(2)
    ring_step(0, 2)
    partial(1, 3)
    partial(1, 5)
    ring_step(1, 1)
    down_second(0)
    up_second(0)
    partial(1, 2)
    partial(1, 6)
    partial(0, 1)
    partial(0, 7)
    ring_step(0, 3)
    down_second(1)
    up_second(1)
    ring_step(1, 2)
    partial(1, 1)
    partial(1, 7)
    partial(0, 0)
    down_second(2)
    up_second(2)
    ring_step(1, 3)
    partial(1, 0)
    ring_last(0)
    down_last(0)
    up_last(0)
    down_last(1)
    up_last(1)
    fin_last(0)
    ring_last(1)
    down_last(2)
    up_last(2)
    fin_last(1)
    for copy in started:
        copy.wait_send()


def hand_over(*refs):
    for i in range(4):
        refs[4 + i][...] = refs[i][...]


def local(
    tokens, cotangent, up_tiles, up_rows, up_columns, up_counts,
    down_tiles, down_rows, down_columns, down_counts,
):
    dma = pltpu.SemaphoreType.DMA
    vm = pltpu.VMEM
    any_space = pl.BlockSpec(memory_space=pl.ANY)
    in_vmem = pl.BlockSpec(memory_space=pltpu.VMEM)
    shapes = (
        jax.ShapeDtypeStruct((ROWS, HALF), BF),
        jax.ShapeDtypeStruct((ROWS, HALF), BF),
        jax.ShapeDtypeStruct((SLOTS, SLICE, BLK), F32),
        jax.ShapeDtypeStruct((SLOTS, SLICE, BLK), F32),
    )
    made = pl.pallas_call(
            kernel,
            out_shape=shapes,
            in_specs=[any_space] * 4 + [pl.BlockSpec(memory_space=pltpu.SMEM)] * 6,
            out_specs=(in_vmem,) * 4,
            scratch_shapes=[
                vm((2, 8, 2, 2, MY_ROWS, HALF), BF),
                vm((SLOTS, BLK, BLK), BF), vm((SLOTS, BLK, BLK), BF),
                vm((SLOTS, BLK, BLK), BF), vm((SLOTS, BLK, BLK), BF),
                vm((8, 128), jnp.int32), vm((8, 128), jnp.int32),
                pltpu.SMEM((2, 8, 128), jnp.int32),
                vm((4, MY_ROWS, BLK), F32),
                vm((4, MY_ROWS, BLK), F32),
                vm((4, MY_ROWS, BLK), BF),
                vm((4, MY_ROWS, BLK), BF),
                vm((8, 2, BLK, MY_ROWS), BF),
                vm((4, BLK, MY_ROWS), BF),
                vm((2, 8, 2, 2, MY_ROWS, HALF), BF),
                vm((2, 8, 2, MY_ROWS, HALF), BF),
                vm((2, 2, 4, 2, MY_ROWS, HALF), BF),
                vm((2, MY_ROWS, HALF), BF),
                vm((GROUPS, 4, 2, 2, PER, SLICE, BLK), BF),
                vm((GROUPS, 2, 2, PER, SLICE, BLK), BF),
                vm((GROUPS, 2, 2, 2, PER, SLICE, BLK), BF),
                vm((GROUPS, 2, 2, PER, SLICE, BLK), BF),
                vm((GROUPS, 3, PER, SLICE, BLK), BF),
                vm((GROUPS, 2, 2, 4, PER, SLICE, BLK), BF),
                vm((GROUPS, 2, 2, PER, SLICE, BLK), BF),
                vm((GROUPS, 2, 4, PER, SLICE, BLK), BF),
                vm((GROUPS, 4, PER, SLICE, BLK), BF),
                vm((GROUPS, 3, PER, SLICE, BLK), BF),
                dma((6,)),
                dma((3,)), dma((3,)),
                dma((2, 2, 4, 2)), dma((2, 2, 4, 2)),
                dma((2, 8)), dma((2, 8)),
                dma((2, 4)), dma((2, 4)),
                dma((2, 8)), dma((2, 8)),
                dma((2, 2, 4, 2)), dma((2, 2, 4, 2)),
                dma((2,)), dma((2,)),
                dma((4, GROUPS, 4)), dma((4, GROUPS, 4)),
            ],
            compiler_params=pltpu.CompilerParams(
                collective_id=0, has_side_effects=True, vmem_limit_bytes=58 << 20
            ),
            name="sparse_feed_forward",
        )(
        tokens, cotangent, up_tiles, down_tiles, up_rows, up_columns, up_counts,
        down_rows, down_columns, down_counts,
    )
    return tuple(
        pl.pallas_call(
            hand_over,
            out_shape=shapes,
            in_specs=[in_vmem] * 4,
            out_specs=(in_vmem,) * 4,
            name="hand_over",
        )(*made)
    )


def solution(mesh):
    return jax.shard_map(
        local,
        mesh=mesh,
        in_specs=(
            P("dp", "mp"),
            P("dp", "mp"),
            P("mp", None, None),
            P("mp"),
            P("mp"),
            P("mp"),
            P("mp", None, None),
            P("mp"),
            P("mp"),
            P("mp"),
        ),
        out_specs=(P("dp", "mp"), P("dp", "mp"), P("mp", "dp", None), P("mp", "dp", None)),
        check_vma=False,
    )
```

```python
import functools
import math

import jax
import jax.numpy as jnp
from jax import lax
from jax.experimental import pallas as pl
from jax.experimental.pallas import tpu as pltpu
from jax.sharding import PartitionSpec as P

BLK = 256
HALF = 128
SLOTS = 12
ROWS = 768
MY_ROWS = 384
GROUPS = 3
PER = SLOTS // GROUPS
SLICE = 32
AT_ONCE = 4
MESH = pl.DeviceIdType.MESH
BF = jnp.bfloat16
F32 = jnp.float32


def pack_pattern(up_rows, up_columns, up_counts, down_rows, down_columns, down_counts):
    lane = lax.broadcasted_iota(jnp.int32, (8, 128), 1)
    row = lax.broadcasted_iota(jnp.int32, (8, 128), 0)
    ups, downs = up_counts[0], down_counts[0]
    packed = jnp.where((row == 6) & (lane == 0), ups, 0)
    packed = jnp.where((row == 6) & (lane == 1), downs, packed)
    for s in range(SLOTS):
        up_row, up_hidden = up_rows[s], up_columns[s] & 1
        down_hidden, down_column = down_rows[s] & 1, down_columns[s]
        up_pair = jnp.where(s < ups, up_hidden * 16 + up_row, -1)
        down_pair = jnp.where(s < downs, down_hidden * 16 + down_column, -1)
        found = ((row == 0) & (lane == up_pair)) | ((row == 1) & (lane == down_pair))
        packed = jnp.where(found, s + 1, packed)
        for at, value in ((2, up_row), (3, up_hidden), (4, down_hidden), (5, down_column)):
            packed = jnp.where((row == at) & (lane == s), value, packed)
    return packed


def kernel(
    tok_in, cot_in, up_in, dn_in, up_rows, up_columns, up_counts, down_rows, down_columns, down_counts,
    mixed_out, tg_out, ug_out, dg_out,
    acts_in, up_own, dn_own, up_other, dn_other, meta_own, meta_v, meta_s, pre, bh, act, slope, tok_t, act_t,
    pbuf, sbuf, rbuf, frecv,
    gd, gda, gdr, gds, gdr2, gu, gua, gur, gus, gur2,
    local_sem, swap_s, swap_r, z_s, z_r, sib_s, sib_r, w_s, w_r,
    rsib_s, rsib_r, ring_s, ring_r, fin_s, fin_r, g_s, g_r,
):
    d = lax.axis_index("dp")
    m = lax.axis_index("mp")
    y = lax.rem(d, 4)
    x_hi = d // 4
    z = m // 4
    x = lax.rem(m // 2, 2)
    c = lax.rem(m, 2)
    other_x = 1 - x
    other_c = 1 - c

    def place(hi, yy, zz, lo, cc):
        return (hi * 4 + yy, zz * 4 + lo * 2 + cc)

    z_next = place(x_hi, y, lax.rem(z + 1, 8), x, c)
    z_prev = place(x_hi, y, lax.rem(z + 7, 8), x, c)
    sibling = place(x_hi, y, z, x, other_c)
    partner = place(x_hi, y, z, other_x, c)
    flip_hi = 1 - x_hi
    x_up = place(lax.rem(x_hi + x, 2), y, z, other_x, c)
    x_down = place(lax.rem(x_hi + other_x, 2), y, z, other_x, c)
    x_peers = [partner, place(flip_hi, y, z, x, c), place(flip_hi, y, z, other_x, c)]
    peer_hi = [x_hi, flip_hi, flip_hi]
    peer_p = [1, 0, 1]
    y_peers = [place(x_hi, lax.rem(y + j, 4), z, x, c) for j in (1, 2, 3)]

    barrier = pltpu.get_barrier_semaphore()
    peers = [z_next, z_prev, sibling] + x_peers + y_peers
    for dev in peers:
        pl.semaphore_signal(barrier, inc=1, device_id=dev, device_id_type=MESH)

    started = []

    def send(src, dst, s, r, dev):
        copy = pltpu.make_async_remote_copy(
            src_ref=src, dst_ref=dst, send_sem=s, recv_sem=r, device_id=dev, device_id_type=MESH
        )
        copy.start()
        started.append(copy)

    def arrived(ref, s, r):
        pltpu.make_async_remote_copy(
            src_ref=ref, dst_ref=ref, send_sem=s, recv_sem=r, device_id=sibling, device_id_type=MESH
        ).wait_recv()

    my_rows = pl.ds(pl.multiple_of(x * MY_ROWS, MY_ROWS), MY_ROWS)
    their_rows = pl.ds(pl.multiple_of(other_x * MY_ROWS, MY_ROWS), MY_ROWS)
    ins = [tok_in, cot_in]
    tiles = [[up_own, up_other], [dn_own, dn_other]]
    locals_ = []
    for a in range(2):
        locals_.append(
            pltpu.make_async_copy(ins[a].at[my_rows], acts_in.at[a, 0, c, x], local_sem.at[a])
        )
    for k, ref in enumerate((up_in, dn_in)):
        locals_.append(
            pltpu.make_async_copy(ref, tiles[k][0], local_sem.at[2 + k])
        )
    for copy in locals_:
        copy.start()
    meta_own[...] = pack_pattern(up_rows, up_columns, up_counts, down_rows, down_columns, down_counts)
    locals_.append(pltpu.make_async_copy(meta_own, meta_s.at[0], local_sem.at[4]))
    locals_[4].start()

    pl.semaphore_wait(barrier, len(peers))

    for a in range(2):
        send(ins[a].at[their_rows], acts_in.at[a, 0, c, x], swap_s.at[a], swap_r.at[a], partner)
    send(meta_own, meta_v, swap_s.at[2], swap_r.at[2], partner)

    def z_send(a, direction, step, block, src, dst):
        send(src, dst, z_s.at[a, direction, step, block], z_r.at[a, direction, step, block],
             z_prev if direction else z_next)

    def z_wait(a, direction, step, block, ref):
        arrived(ref, z_s.at[a, direction, step, block], z_r.at[a, direction, step, block])

    def sib_send(a, r):
        ref = acts_in.at[a, r, c]
        send(ref, ref, sib_s.at[a, r], sib_r.at[a, r], sibling)

    def sib_wait(a, r):
        arrived(acts_in.at[a, r, other_c], sib_s.at[a, r], sib_r.at[a, r])

    def quarter(i):
        return pl.ds(3 * lax.rem(y + i, 4), 3)

    def send_own(a):
        locals_[a].wait()
        for direction, r in ((0, 1), (1, 7)):
            z_send(a, direction, 0, x, acts_in.at[a, 0, c, x], acts_in.at[a, r, c, x])

    def swap_done(a):
        arrived(acts_in.at[a, 0, c, other_x], swap_s.at[a], swap_r.at[a])
        sib_send(a, 0)

    def send_swapped(a):
        for direction, r in ((0, 1), (1, 7)):
            z_send(a, direction, 0, other_x, acts_in.at[a, 0, c, other_x], acts_in.at[a, r, c, other_x])

    send_own(0)
    for k in range(2):
        locals_[2 + k].wait()
        for i, dev in ((0, x_up), (1, x_down)):
            send(tiles[k][0].at[quarter(i)], tiles[k][1].at[quarter(i)], w_s.at[k, i], w_r.at[k, i], dev)
    swap_done(0)
    send_swapped(0)
    send_own(1)
    locals_[4].wait()
    arrived(meta_v, swap_s.at[2], swap_r.at[2])
    to_smem = pltpu.make_async_copy(meta_v, meta_s.at[1], local_sem.at[5])
    to_smem.start()
    swap_done(1)

    def tile(kind, p, h, b):
        found = meta_s[p, kind, h * 16 + b]
        value = tiles[kind][p][jnp.maximum(found - 1, 0)]
        return jnp.where(found > 0, value, jnp.zeros_like(value))

    def pass_weights(k):
        for i, j, dev in ((0, 3, y_peers[0]), (1, 2, y_peers[2])):
            ref = tiles[k][1].at[quarter(i)]
            arrived(ref, w_s.at[k, i], w_r.at[k, i])
            send(ref, ref, w_s.at[k, j], w_r.at[k, j], dev)

    def rest_of_weights(k):
        for j in (2, 3):
            arrived(tiles[k][1].at[quarter(j)], w_s.at[k, j], w_r.at[k, j])

    sums = [pre, bh]

    def accumulate(a, p, r, first):
        left = jnp.concatenate(
            [acts_in[a, r, 0, 0], acts_in[a, r, 1, 0], acts_in[a, r, 0, 1], acts_in[a, r, 1, 1]], axis=1
        )
        if a == 0 and p == 0:
            for xx in range(2):
                tok_t[r, xx] = left[:, xx * BLK:(xx + 1) * BLK].T
        b = 2 * lax.rem(z + 8 - r, 8)
        for h in range(2):
            w0, w1 = tile(a, p, h, b), tile(a, p, h, b + 1)
            if a == 0:
                out = jnp.dot(left, jnp.concatenate([w0, w1], axis=0), preferred_element_type=F32)
            else:
                out = lax.dot_general(
                    left, jnp.concatenate([w0, w1], axis=1), (((1,), (1,)), ((), ())),
                    preferred_element_type=F32,
                )
            if first:
                sums[a][p * 2 + h] = out
            else:
                sums[a][p * 2 + h] += out

    def forward(a, k):
        for block in (x, other_x):
            for direction, r in ((0, k), (1, 8 - k)):
                z_wait(a, direction, k - 1, block, acts_in.at[a, r, c, block])
                if k < 3:
                    z_send(a, direction, k, block, acts_in.at[a, r, c, block],
                           acts_in.at[a, r + 1 - 2 * direction, c, block])
        for direction, r in ((0, k), (1, 8 - k)):
            if k == 3:
                z_send(a, direction, 3, direction, acts_in.at[a, r, c, direction],
                       acts_in.at[a, 4, c, direction])
            sib_send(a, r)

    def last_unit(a):
        for direction in range(2):
            z_wait(a, direction, 3, direction, acts_in.at[a, 4, c, direction])
        sib_send(a, 4)

    def own_products(a, units):
        for r in units:
            sib_wait(a, r)
            accumulate(a, 0, r, r == 0)

    def other_products(a):
        accumulate(a, 1, 0, True)

        def rest(r, carry):
            accumulate(a, 1, r, False)
            return carry

        lax.fori_loop(1, 8, rest, 0)

    def gelu_step(i, carry):
        h = i // 6
        rows = pl.ds(pl.multiple_of(lax.rem(i, 6) * 64, 64), 64)
        v = pre[h, rows]
        cdf = 0.5 * (1.0 + lax.erf(v * 0.7071067811865476))
        act[h, rows] = (v * cdf).astype(BF)
        pre[h, rows] = cdf + v * jnp.exp(-0.5 * v * v) * 0.3989422804014327
        return carry

    def slope_step(i, carry):
        h = i // 6
        rows = pl.ds(pl.multiple_of(lax.rem(i, 6) * 64, 64), 64)
        slope[h, rows] = (bh[h, rows] * pre[h, rows]).astype(BF)
        return carry

    lefts = [act, slope]

    def partial(o, q):
        left = jnp.concatenate([lefts[o][h] for h in range(4)], axis=1)
        b = 2 * lax.rem(z + q, 8)
        kind = 1 - o
        for xx in range(2):
            ws = [tile(kind, h // 2, h % 2, b + xx) for h in range(4)]
            if o == 0:
                out = jnp.dot(left, jnp.concatenate(ws, axis=0), preferred_element_type=F32)
            else:
                out = lax.dot_general(
                    left, jnp.concatenate(ws, axis=1), (((1,), (1,)), ((), ())),
                    preferred_element_type=F32,
                )
            out = out.astype(BF)
            for half in range(2):
                pbuf[o, q, half, xx] = out[:, half * HALF:(half + 1) * HALF]
        send(pbuf.at[o, q, other_c], sbuf.at[o, q], rsib_s.at[o, q], rsib_r.at[o, q], sibling)

    def sibling_part(o, q):
        arrived(sbuf.at[o, q], rsib_s.at[o, q], rsib_r.at[o, q])

    def add(o, q, xx, came):
        total = pbuf[o, q, c, xx].astype(F32) + sbuf[o, q, xx].astype(F32)
        for ref in came:
            total += ref[...].astype(F32)
        pbuf[o, q, c, xx] = total.astype(BF)

    def ring_send(o, direction, step, xx):
        q = 4 + step if direction else 4 - step
        send(pbuf.at[o, q, c, xx], rbuf.at[o, direction, step, xx],
             ring_s.at[o, direction, step, xx], ring_r.at[o, direction, step, xx],
             z_prev if direction else z_next)

    def ring_wait(o, direction, step, xx):
        ref = rbuf.at[o, direction, step, xx]
        arrived(ref, ring_s.at[o, direction, step, xx], ring_r.at[o, direction, step, xx])
        return ref

    def ring_first(o):
        sibling_part(o, 4)
        for direction in range(2):
            add(o, 4, direction, [])
            ring_send(o, direction, 0, direction)

    def ring_step(o, step):
        for q in (4 - step, 4 + step):
            sibling_part(o, q)
        if step == 1:
            for direction in range(2):
                add(o, 4 + step if direction else 4 - step, 1 - direction, [])
                ring_send(o, direction, step, 1 - direction)
            for direction in range(2):
                came = ring_wait(o, direction, 0, direction)
                add(o, 4 + step if direction else 4 - step, direction, [came])
                ring_send(o, direction, step, direction)
            return
        for xx in (other_x, x):
            for direction in range(2):
                came = ring_wait(o, direction, step - 1, xx)
                add(o, 4 + step if direction else 4 - step, xx, [came])
                ring_send(o, direction, step, xx)

    outs = [mixed_out, tg_out]

    def ring_last(o):
        sibling_part(o, 0)
        for xx in (other_x, x):
            add(o, 0, xx, [ring_wait(o, direction, 3, xx) for direction in range(2)])
            if xx is other_x:
                send(pbuf.at[o, 0, c, other_x], frecv.at[o], fin_s.at[o], fin_r.at[o], partner)
        outs[o][my_rows] = pbuf[o, 0, c, x]

    def gelu():
        lax.fori_loop(0, 24, gelu_step, 0)

    def slopes():
        lax.fori_loop(0, 24, slope_step, 0)

    def turn():
        for h in range(4):
            act_t[h] = act[h].T

    def fin_last(o):
        arrived(frecv.at[o], fin_s.at[o], fin_r.at[o])
        outs[o][their_rows] = frecv[o]

    scale = 1.0 / math.sqrt(ROWS * 8)

    def grad_product(kind, p, i):
        if kind == 0:
            block, h = meta_s[p, 2, i], meta_s[p, 3, i]
        else:
            block, h = meta_s[p, 5, i], meta_s[p, 4, i]
        r = lax.rem(z + 8 - block // 2, 8)
        xx = lax.rem(block, 2)
        if kind == 0:
            left, right = tok_t[r, xx], slope[p * 2 + h]
        else:
            left = act_t[p * 2 + h]
            right = jnp.concatenate([acts_in[1, r, 0, xx], acts_in[1, r, 1, xx]], axis=1)
        out = jnp.dot(left, right, preferred_element_type=F32)
        live = jnp.where(i < meta_s[p, 6, kind], scale, 0.0)
        return (out * live).astype(BF)

    y_next, y_next2, y_prev = (lax.rem(y + j, 4) for j in (1, 2, 3))
    up_hi, down_hi = lax.rem(x_hi + x, 2), lax.rem(x_hi + other_x, 2)

    def grad_send(kind, g, i, src, dst, dev):
        send(src, dst, g_s.at[kind, g, i], g_r.at[kind, g, i], dev)

    def grad_wait(kind, g, i, ref):
        arrived(ref, g_s.at[kind, g, i], g_r.at[kind, g, i])

    def down_group(g):
        def some(t, carry):
            for n in range(AT_ONCE):
                p, i = n % 2, t * (AT_ONCE // 2) + n // 2
                out = grad_product(1, p, g * PER + i)
                for part in range(8):
                    gd[g, part % 4, part // 4, p, i] = out[part * SLICE:(part + 1) * SLICE]
            return carry

        lax.fori_loop(0, 2 * PER // AT_ONCE, some, 0)
        grad_send(0, g, 0, gd.at[g, y_next2, 0], gda.at[g, 0], y_peers[0])
        grad_send(0, g, 1, gd.at[g, y_next2, 1], gda.at[g, 1], y_peers[2])

    def down_mid(g):
        for i, to, hi, dev in ((0, y_next, 0, y_peers[0]), (1, y_prev, 1, y_peers[2])):
            grad_wait(0, g, i, gda.at[g, i])
            for p in range(2):
                gd[g, to, hi, p] = (gd[g, to, hi, p].astype(F32) + gda[g, i, p].astype(F32)).astype(BF)
            grad_send(0, g, 2 + i, gd.at[g, to], gdr.at[g, i], dev)

    def up_group(g):
        def some(t, carry):
            for n in range(AT_ONCE):
                p, i = n % 2, t * (AT_ONCE // 2) + n // 2
                out = grad_product(0, p, g * PER + i)
                for part in range(8):
                    gu[g, part // 4, p, part % 4, i] = out[part * SLICE:(part + 1) * SLICE]
            return carry

        lax.fori_loop(0, 2 * PER // AT_ONCE, some, 0)
        low, high = pl.ds(0, 2), pl.ds(2, 2)
        grad_send(1, g, 0, gu.at[g, flip_hi, 0, low], gua.at[g, 0], x_up)
        grad_send(1, g, 1, gu.at[g, flip_hi, 0, high], gua.at[g, 1], x_down)

    def up_mid(g):
        for i, hi, dev in ((0, up_hi, x_up), (1, down_hi, x_down)):
            grad_wait(1, g, i, gua.at[g, i])
            for yy in range(2):
                both = gu[g, hi, 1, 2 * i + yy].astype(F32) + gua[g, i, yy].astype(F32)
                gu[g, hi, 1, 2 * i + yy] = both.astype(BF)
            grad_send(1, g, 2 + i, gu.at[g, hi, 1], gur.at[g, i], dev)

    def down_second(g):
        for i in range(2):
            grad_wait(0, g, 2 + i, gdr.at[g, i])
        for hi in range(2):
            for p in range(2):
                total = gd[g, y, hi, p].astype(F32)
                for i in range(2):
                    total += gdr[g, i, hi, p].astype(F32)
                gds[g, hi, p] = total.astype(BF)
        for j in range(3):
            grad_send(2, g, j, gds.at[g, peer_hi[j], peer_p[j]], gdr2.at[g, j], x_peers[j])

    def up_second(g):
        for i in range(2):
            grad_wait(1, g, 2 + i, gur.at[g, i])
        for yy in range(4):
            total = gu[g, x_hi, 0, yy].astype(F32)
            for i in range(2):
                total += gur[g, i, yy].astype(F32)
            gus[g, yy] = total.astype(BF)
        for j in range(3):
            grad_send(3, g, j, gus.at[g, lax.rem(y + j + 1, 4)], gur2.at[g, j], y_peers[j])

    def down_last(g):
        for j in range(3):
            grad_wait(2, g, j, gdr2.at[g, j])
        total = gds[g, x_hi, 0].astype(F32)
        for j in range(3):
            total += gdr2[g, j].astype(F32)
        dg_out[g * PER:(g + 1) * PER] = total

    def up_last(g):
        for j in range(3):
            grad_wait(3, g, j, gur2.at[g, j])
        total = gus[g, y].astype(F32)
        for j in range(3):
            total += gur2[g, j].astype(F32)
        ug_out[g * PER:(g + 1) * PER] = total

    send_swapped(1)
    forward(0, 1)
    own_products(0, (0,))
    forward(1, 1)
    pass_weights(0)
    own_products(0, (1, 7))
    forward(0, 2)
    own_products(1, (0,))
    forward(1, 2)
    own_products(0, (2, 6))
    pass_weights(1)
    forward(0, 3)
    own_products(1, (1, 7))
    to_smem.wait()
    forward(1, 3)
    last_unit(0)
    own_products(0, (3, 5))
    rest_of_weights(0)
    own_products(0, (4,))
    other_products(0)
    gelu()
    turn()
    rest_of_weights(1)
    partial(0, 4)
    partial(0, 3)
    ring_first(0)
    own_products(1, (2, 6))
    partial(0, 5)
    accumulate(1, 1, 0, True)
    accumulate(1, 1, 1, False)
    accumulate(1, 1, 7, False)
    accumulate(1, 1, 2, False)
    accumulate(1, 1, 6, False)
    last_unit(1)
    own_products(1, (3, 5))
    accumulate(1, 1, 3, False)
    accumulate(1, 1, 5, False)
    sib_wait(1, 4)
    down_group(0)
    accumulate(1, 0, 4, False)
    accumulate(1, 1, 4, False)
    slopes()
    up_group(0)
    down_group(1)
    ring_step(0, 1)
    up_group(1)
    down_group(2)
    down_mid(0)
    up_mid(0)
    up_group(2)
    partial(1, 4)
    down_mid(1)
    up_mid(1)
    ring_first(1)
    partial(0, 2)
    partial(0, 6)
    down_mid(2)
    up_mid(2)
    ring_step(0, 2)
    partial(1, 3)
    partial(1, 5)
    ring_step(1, 1)
    down_second(0)
    up_second(0)
    partial(1, 2)
    partial(1, 6)
    partial(0, 1)
    partial(0, 7)
    ring_step(0, 3)
    down_second(1)
    up_second(1)
    ring_step(1, 2)
    partial(1, 1)
    partial(1, 7)
    partial(0, 0)
    down_second(2)
    up_second(2)
    ring_step(1, 3)
    partial(1, 0)
    ring_last(0)
    down_last(0)
    up_last(0)
    down_last(1)
    up_last(1)
    fin_last(0)
    ring_last(1)
    down_last(2)
    up_last(2)
    fin_last(1)
    for copy in started:
        copy.wait_send()


def hand_over(*refs):
    for i in range(4):
        refs[4 + i][...] = refs[i][...]


def local(
    tokens, cotangent, up_tiles, up_rows, up_columns, up_counts,
    down_tiles, down_rows, down_columns, down_counts,
):
    dma = pltpu.SemaphoreType.DMA
    vm = pltpu.VMEM
    any_space = pl.BlockSpec(memory_space=pl.ANY)
    in_vmem = pl.BlockSpec(memory_space=pltpu.VMEM)
    shapes = (
        jax.ShapeDtypeStruct((ROWS, HALF), BF),
        jax.ShapeDtypeStruct((ROWS, HALF), BF),
        jax.ShapeDtypeStruct((SLOTS, SLICE, BLK), F32),
        jax.ShapeDtypeStruct((SLOTS, SLICE, BLK), F32),
    )
    made = pl.pallas_call(
            kernel,
            out_shape=shapes,
            in_specs=[any_space] * 4 + [pl.BlockSpec(memory_space=pltpu.SMEM)] * 6,
            out_specs=(in_vmem,) * 4,
            scratch_shapes=[
                vm((2, 8, 2, 2, MY_ROWS, HALF), BF),
                vm((SLOTS, BLK, BLK), BF), vm((SLOTS, BLK, BLK), BF),
                vm((SLOTS, BLK, BLK), BF), vm((SLOTS, BLK, BLK), BF),
                vm((8, 128), jnp.int32), vm((8, 128), jnp.int32),
                pltpu.SMEM((2, 8, 128), jnp.int32),
                vm((4, MY_ROWS, BLK), F32),
                vm((4, MY_ROWS, BLK), F32),
                vm((4, MY_ROWS, BLK), BF),
                vm((4, MY_ROWS, BLK), BF),
                vm((8, 2, BLK, MY_ROWS), BF),
                vm((4, BLK, MY_ROWS), BF),
                vm((2, 8, 2, 2, MY_ROWS, HALF), BF),
                vm((2, 8, 2, MY_ROWS, HALF), BF),
                vm((2, 2, 4, 2, MY_ROWS, HALF), BF),
                vm((2, MY_ROWS, HALF), BF),
                vm((GROUPS, 4, 2, 2, PER, SLICE, BLK), BF),
                vm((GROUPS, 2, 2, PER, SLICE, BLK), BF),
                vm((GROUPS, 2, 2, 2, PER, SLICE, BLK), BF),
                vm((GROUPS, 2, 2, PER, SLICE, BLK), BF),
                vm((GROUPS, 3, PER, SLICE, BLK), BF),
                vm((GROUPS, 2, 2, 4, PER, SLICE, BLK), BF),
                vm((GROUPS, 2, 2, PER, SLICE, BLK), BF),
                vm((GROUPS, 2, 4, PER, SLICE, BLK), BF),
                vm((GROUPS, 4, PER, SLICE, BLK), BF),
                vm((GROUPS, 3, PER, SLICE, BLK), BF),
                dma((6,)),
                dma((3,)), dma((3,)),
                dma((2, 2, 4, 2)), dma((2, 2, 4, 2)),
                dma((2, 8)), dma((2, 8)),
                dma((2, 4)), dma((2, 4)),
                dma((2, 8)), dma((2, 8)),
                dma((2, 2, 4, 2)), dma((2, 2, 4, 2)),
                dma((2,)), dma((2,)),
                dma((4, GROUPS, 4)), dma((4, GROUPS, 4)),
            ],
            compiler_params=pltpu.CompilerParams(
                collective_id=0, has_side_effects=True, vmem_limit_bytes=58 << 20
            ),
            name="sparse_feed_forward",
        )(
        tokens, cotangent, up_tiles, down_tiles, up_rows, up_columns, up_counts,
        down_rows, down_columns, down_counts,
    )
    return tuple(
        pl.pallas_call(
            hand_over,
            out_shape=shapes,
            in_specs=[in_vmem] * 4,
            out_specs=(in_vmem,) * 4,
            name="hand_over",
        )(*made)
    )


def solution(mesh):
    return jax.shard_map(
        local,
        mesh=mesh,
        in_specs=(
            P("dp", "mp"),
            P("dp", "mp"),
            P("mp", None, None),
            P("mp"),
            P("mp"),
            P("mp"),
            P("mp", None, None),
            P("mp"),
            P("mp"),
            P("mp"),
        ),
        out_specs=(P("dp", "mp"), P("dp", "mp"), P("mp", "dp", None), P("mp", "dp", None)),
        check_vma=False,
    )
```

```python
import functools
import math

import jax
import jax.numpy as jnp
from jax import lax
from jax.experimental import pallas as pl
from jax.experimental.pallas import tpu as pltpu
from jax.sharding import PartitionSpec as P

BLK = 256
HALF = 128
SLOTS = 12
ROWS = 768
MY_ROWS = 384
GROUPS = 3
PER = SLOTS // GROUPS
SLICE = 32
AT_ONCE = 4
MESH = pl.DeviceIdType.MESH
BF = jnp.bfloat16
F32 = jnp.float32


def pack_pattern(up_rows, up_columns, up_counts, down_rows, down_columns, down_counts):
    lane = lax.broadcasted_iota(jnp.int32, (8, 128), 1)
    row = lax.broadcasted_iota(jnp.int32, (8, 128), 0)
    ups, downs = up_counts[0], down_counts[0]
    packed = jnp.where((row == 6) & (lane == 0), ups, 0)
    packed = jnp.where((row == 6) & (lane == 1), downs, packed)
    for s in range(SLOTS):
        up_row, up_hidden = up_rows[s], up_columns[s] & 1
        down_hidden, down_column = down_rows[s] & 1, down_columns[s]
        up_pair = jnp.where(s < ups, up_hidden * 16 + up_row, -1)
        down_pair = jnp.where(s < downs, down_hidden * 16 + down_column, -1)
        found = ((row == 0) & (lane == up_pair)) | ((row == 1) & (lane == down_pair))
        packed = jnp.where(found, s + 1, packed)
        for at, value in ((2, up_row), (3, up_hidden), (4, down_hidden), (5, down_column)):
            packed = jnp.where((row == at) & (lane == s), value, packed)
    return packed


def kernel(
    tok_in, cot_in, up_in, dn_in, up_rows, up_columns, up_counts, down_rows, down_columns, down_counts,
    mixed_out, tg_out, ug_out, dg_out,
    acts_in, up_own, dn_own, up_other, dn_other, meta_own, meta_v, meta_s, pre, bh, act, slope, tok_t, act_t,
    pbuf, sbuf, rbuf, frecv,
    gd, gda, gdr, gds, gdr2, gu, gua, gur, gus, gur2,
    local_sem, swap_s, swap_r, z_s, z_r, sib_s, sib_r, w_s, w_r,
    rsib_s, rsib_r, ring_s, ring_r, fin_s, fin_r, g_s, g_r,
):
    d = lax.axis_index("dp")
    m = lax.axis_index("mp")
    y = lax.rem(d, 4)
    x_hi = d // 4
    z = m // 4
    x = lax.rem(m // 2, 2)
    c = lax.rem(m, 2)
    other_x = 1 - x
    other_c = 1 - c

    def place(hi, yy, zz, lo, cc):
        return (hi * 4 + yy, zz * 4 + lo * 2 + cc)

    z_next = place(x_hi, y, lax.rem(z + 1, 8), x, c)
    z_prev = place(x_hi, y, lax.rem(z + 7, 8), x, c)
    sibling = place(x_hi, y, z, x, other_c)
    partner = place(x_hi, y, z, other_x, c)
    flip_hi = 1 - x_hi
    x_up = place(lax.rem(x_hi + x, 2), y, z, other_x, c)
    x_down = place(lax.rem(x_hi + other_x, 2), y, z, other_x, c)
    x_peers = [partner, place(flip_hi, y, z, x, c), place(flip_hi, y, z, other_x, c)]
    peer_hi = [x_hi, flip_hi, flip_hi]
    peer_p = [1, 0, 1]
    y_peers = [place(x_hi, lax.rem(y + j, 4), z, x, c) for j in (1, 2, 3)]

    barrier = pltpu.get_barrier_semaphore()
    peers = [z_next, z_prev, sibling] + x_peers + y_peers
    for dev in peers:
        pl.semaphore_signal(barrier, inc=1, device_id=dev, device_id_type=MESH)

    started = []

    def send(src, dst, s, r, dev):
        copy = pltpu.make_async_remote_copy(
            src_ref=src, dst_ref=dst, send_sem=s, recv_sem=r, device_id=dev, device_id_type=MESH
        )
        copy.start()
        started.append(copy)

    def arrived(ref, s, r):
        pltpu.make_async_remote_copy(
            src_ref=ref, dst_ref=ref, send_sem=s, recv_sem=r, device_id=sibling, device_id_type=MESH
        ).wait_recv()

    my_rows = pl.ds(pl.multiple_of(x * MY_ROWS, MY_ROWS), MY_ROWS)
    their_rows = pl.ds(pl.multiple_of(other_x * MY_ROWS, MY_ROWS), MY_ROWS)
    ins = [tok_in, cot_in]
    tiles = [[up_own, up_other], [dn_own, dn_other]]
    locals_ = []
    for a in range(2):
        locals_.append(
            pltpu.make_async_copy(ins[a].at[my_rows], acts_in.at[a, 0, c, x], local_sem.at[a])
        )
    for k, ref in enumerate((up_in, dn_in)):
        locals_.append(
            pltpu.make_async_copy(ref, tiles[k][0], local_sem.at[2 + k])
        )
    for copy in locals_:
        copy.start()
    meta_own[...] = pack_pattern(up_rows, up_columns, up_counts, down_rows, down_columns, down_counts)
    locals_.append(pltpu.make_async_copy(meta_own, meta_s.at[0], local_sem.at[4]))
    locals_[4].start()

    pl.semaphore_wait(barrier, len(peers))

    for a in range(2):
        send(ins[a].at[their_rows], acts_in.at[a, 0, c, x], swap_s.at[a], swap_r.at[a], partner)
    send(meta_own, meta_v, swap_s.at[2], swap_r.at[2], partner)

    def z_send(a, direction, step, block, src, dst):
        send(src, dst, z_s.at[a, direction, step, block], z_r.at[a, direction, step, block],
             z_prev if direction else z_next)

    def z_wait(a, direction, step, block, ref):
        arrived(ref, z_s.at[a, direction, step, block], z_r.at[a, direction, step, block])

    def sib_send(a, r):
        ref = acts_in.at[a, r, c]
        send(ref, ref, sib_s.at[a, r], sib_r.at[a, r], sibling)

    def sib_wait(a, r):
        arrived(acts_in.at[a, r, other_c], sib_s.at[a, r], sib_r.at[a, r])

    def quarter(i):
        return pl.ds(3 * lax.rem(y + i, 4), 3)

    def send_own(a):
        locals_[a].wait()
        for direction, r in ((0, 1), (1, 7)):
            z_send(a, direction, 0, x, acts_in.at[a, 0, c, x], acts_in.at[a, r, c, x])

    def swap_done(a):
        arrived(acts_in.at[a, 0, c, other_x], swap_s.at[a], swap_r.at[a])
        sib_send(a, 0)

    def send_swapped(a):
        for direction, r in ((0, 1), (1, 7)):
            z_send(a, direction, 0, other_x, acts_in.at[a, 0, c, other_x], acts_in.at[a, r, c, other_x])

    send_own(0)
    for k in range(2):
        locals_[2 + k].wait()
        for i, dev in ((0, x_up), (1, x_down)):
            send(tiles[k][0].at[quarter(i)], tiles[k][1].at[quarter(i)], w_s.at[k, i], w_r.at[k, i], dev)
    swap_done(0)
    send_swapped(0)
    send_own(1)
    locals_[4].wait()
    arrived(meta_v, swap_s.at[2], swap_r.at[2])
    to_smem = pltpu.make_async_copy(meta_v, meta_s.at[1], local_sem.at[5])
    to_smem.start()
    swap_done(1)

    def tile(kind, p, h, b):
        found = meta_s[p, kind, h * 16 + b]
        value = tiles[kind][p][jnp.maximum(found - 1, 0)]
        return jnp.where(found > 0, value, jnp.zeros_like(value))

    def pass_weights(k):
        for i, j, dev in ((0, 3, y_peers[0]), (1, 2, y_peers[2])):
            ref = tiles[k][1].at[quarter(i)]
            arrived(ref, w_s.at[k, i], w_r.at[k, i])
            send(ref, ref, w_s.at[k, j], w_r.at[k, j], dev)

    def rest_of_weights(k):
        for j in (2, 3):
            arrived(tiles[k][1].at[quarter(j)], w_s.at[k, j], w_r.at[k, j])

    sums = [pre, bh]

    def accumulate(a, p, r, first):
        left = jnp.concatenate(
            [acts_in[a, r, 0, 0], acts_in[a, r, 1, 0], acts_in[a, r, 0, 1], acts_in[a, r, 1, 1]], axis=1
        )
        if a == 0 and p == 0:
            for xx in range(2):
                tok_t[r, xx] = left[:, xx * BLK:(xx + 1) * BLK].T
        b = 2 * lax.rem(z + 8 - r, 8)
        for h in range(2):
            w0, w1 = tile(a, p, h, b), tile(a, p, h, b + 1)
            if a == 0:
                out = jnp.dot(left, jnp.concatenate([w0, w1], axis=0), preferred_element_type=F32)
            else:
                out = lax.dot_general(
                    left, jnp.concatenate([w0, w1], axis=1), (((1,), (1,)), ((), ())),
                    preferred_element_type=F32,
                )
            if first:
                sums[a][p * 2 + h] = out
            else:
                sums[a][p * 2 + h] += out

    def forward(a, k):
        for block in (x, other_x):
            for direction, r in ((0, k), (1, 8 - k)):
                z_wait(a, direction, k - 1, block, acts_in.at[a, r, c, block])
                if k < 3:
                    z_send(a, direction, k, block, acts_in.at[a, r, c, block],
                           acts_in.at[a, r + 1 - 2 * direction, c, block])
        for direction, r in ((0, k), (1, 8 - k)):
            if k == 3:
                z_send(a, direction, 3, direction, acts_in.at[a, r, c, direction],
                       acts_in.at[a, 4, c, direction])
            sib_send(a, r)

    def last_unit(a):
        for direction in range(2):
            z_wait(a, direction, 3, direction, acts_in.at[a, 4, c, direction])
        sib_send(a, 4)

    def own_products(a, units):
        for r in units:
            sib_wait(a, r)
            accumulate(a, 0, r, r == 0)

    def other_products(a):
        for r in range(8):
            accumulate(a, 1, r, r == 0)

    def gelu_step(i, carry):
        h = i // 6
        rows = pl.ds(pl.multiple_of(lax.rem(i, 6) * 64, 64), 64)
        v = pre[h, rows]
        cdf = 0.5 * (1.0 + lax.erf(v * 0.7071067811865476))
        act[h, rows] = (v * cdf).astype(BF)
        pre[h, rows] = cdf + v * jnp.exp(-0.5 * v * v) * 0.3989422804014327
        return carry

    def slope_step(i, carry):
        h = i // 6
        rows = pl.ds(pl.multiple_of(lax.rem(i, 6) * 64, 64), 64)
        slope[h, rows] = (bh[h, rows] * pre[h, rows]).astype(BF)
        return carry

    lefts = [act, slope]

    def partial(o, q):
        left = jnp.concatenate([lefts[o][h] for h in range(4)], axis=1)
        b = 2 * lax.rem(z + q, 8)
        kind = 1 - o
        for xx in range(2):
            ws = [tile(kind, h // 2, h % 2, b + xx) for h in range(4)]
            if o == 0:
                out = jnp.dot(left, jnp.concatenate(ws, axis=0), preferred_element_type=F32)
            else:
                out = lax.dot_general(
                    left, jnp.concatenate(ws, axis=1), (((1,), (1,)), ((), ())),
                    preferred_element_type=F32,
                )
            out = out.astype(BF)
            for half in range(2):
                pbuf[o, q, half, xx] = out[:, half * HALF:(half + 1) * HALF]
        send(pbuf.at[o, q, other_c], sbuf.at[o, q], rsib_s.at[o, q], rsib_r.at[o, q], sibling)

    def sibling_part(o, q):
        arrived(sbuf.at[o, q], rsib_s.at[o, q], rsib_r.at[o, q])

    def add(o, q, xx, came):
        total = pbuf[o, q, c, xx].astype(F32) + sbuf[o, q, xx].astype(F32)
        for ref in came:
            total += ref[...].astype(F32)
        pbuf[o, q, c, xx] = total.astype(BF)

    def ring_send(o, direction, step, xx):
        q = 4 + step if direction else 4 - step
        send(pbuf.at[o, q, c, xx], rbuf.at[o, direction, step, xx],
             ring_s.at[o, direction, step, xx], ring_r.at[o, direction, step, xx],
             z_prev if direction else z_next)

    def ring_wait(o, direction, step, xx):
        ref = rbuf.at[o, direction, step, xx]
        arrived(ref, ring_s.at[o, direction, step, xx], ring_r.at[o, direction, step, xx])
        return ref

    def ring_first(o):
        sibling_part(o, 4)
        for direction in range(2):
            add(o, 4, direction, [])
            ring_send(o, direction, 0, direction)

    def ring_step(o, step):
        for q in (4 - step, 4 + step):
            sibling_part(o, q)
        if step == 1:
            for direction in range(2):
                add(o, 4 + step if direction else 4 - step, 1 - direction, [])
                ring_send(o, direction, step, 1 - direction)
            for direction in range(2):
                came = ring_wait(o, direction, 0, direction)
                add(o, 4 + step if direction else 4 - step, direction, [came])
                ring_send(o, direction, step, direction)
            return
        for xx in (other_x, x):
            for direction in range(2):
                came = ring_wait(o, direction, step - 1, xx)
                add(o, 4 + step if direction else 4 - step, xx, [came])
                ring_send(o, direction, step, xx)

    outs = [mixed_out, tg_out]

    def ring_last(o):
        sibling_part(o, 0)
        for xx in (other_x, x):
            add(o, 0, xx, [ring_wait(o, direction, 3, xx) for direction in range(2)])
            if xx is other_x:
                send(pbuf.at[o, 0, c, other_x], frecv.at[o], fin_s.at[o], fin_r.at[o], partner)
        outs[o][my_rows] = pbuf[o, 0, c, x]

    def gelu():
        lax.fori_loop(0, 24, gelu_step, 0)

    def slopes():
        lax.fori_loop(0, 24, slope_step, 0)

    def turn():
        for h in range(4):
            act_t[h] = act[h].T

    def fin_last(o):
        arrived(frecv.at[o], fin_s.at[o], fin_r.at[o])
        outs[o][their_rows] = frecv[o]

    scale = 1.0 / math.sqrt(ROWS * 8)

    def grad_product(kind, p, i):
        if kind == 0:
            block, h = meta_s[p, 2, i], meta_s[p, 3, i]
        else:
            block, h = meta_s[p, 5, i], meta_s[p, 4, i]
        r = lax.rem(z + 8 - block // 2, 8)
        xx = lax.rem(block, 2)
        if kind == 0:
            left, right = tok_t[r, xx], slope[p * 2 + h]
        else:
            left = act_t[p * 2 + h]
            right = jnp.concatenate([acts_in[1, r, 0, xx], acts_in[1, r, 1, xx]], axis=1)
        out = jnp.dot(left, right, preferred_element_type=F32)
        live = jnp.where(i < meta_s[p, 6, kind], scale, 0.0)
        return (out * live).astype(BF)

    y_next, y_next2, y_prev = (lax.rem(y + j, 4) for j in (1, 2, 3))
    up_hi, down_hi = lax.rem(x_hi + x, 2), lax.rem(x_hi + other_x, 2)

    def grad_send(kind, g, i, src, dst, dev):
        send(src, dst, g_s.at[kind, g, i], g_r.at[kind, g, i], dev)

    def grad_wait(kind, g, i, ref):
        arrived(ref, g_s.at[kind, g, i], g_r.at[kind, g, i])

    def down_group(g):
        def some(t, carry):
            for n in range(AT_ONCE):
                p, i = n % 2, t * (AT_ONCE // 2) + n // 2
                out = grad_product(1, p, g * PER + i)
                for part in range(8):
                    gd[g, part % 4, part // 4, p, i] = out[part * SLICE:(part + 1) * SLICE]
            return carry

        lax.fori_loop(0, 2 * PER // AT_ONCE, some, 0)
        grad_send(0, g, 0, gd.at[g, y_next2, 0], gda.at[g, 0], y_peers[0])
        grad_send(0, g, 1, gd.at[g, y_next2, 1], gda.at[g, 1], y_peers[2])

    def down_mid(g):
        for i, to, hi, dev in ((0, y_next, 0, y_peers[0]), (1, y_prev, 1, y_peers[2])):
            grad_wait(0, g, i, gda.at[g, i])
            for p in range(2):
                gd[g, to, hi, p] = (gd[g, to, hi, p].astype(F32) + gda[g, i, p].astype(F32)).astype(BF)
            grad_send(0, g, 2 + i, gd.at[g, to], gdr.at[g, i], dev)

    def up_group(g):
        def some(t, carry):
            for n in range(AT_ONCE):
                p, i = n % 2, t * (AT_ONCE // 2) + n // 2
                out = grad_product(0, p, g * PER + i)
                for part in range(8):
                    gu[g, part // 4, p, part % 4, i] = out[part * SLICE:(part + 1) * SLICE]
            return carry

        lax.fori_loop(0, 2 * PER // AT_ONCE, some, 0)
        low, high = pl.ds(0, 2), pl.ds(2, 2)
        grad_send(1, g, 0, gu.at[g, flip_hi, 0, low], gua.at[g, 0], x_up)
        grad_send(1, g, 1, gu.at[g, flip_hi, 0, high], gua.at[g, 1], x_down)

    def up_mid(g):
        for i, hi, dev in ((0, up_hi, x_up), (1, down_hi, x_down)):
            grad_wait(1, g, i, gua.at[g, i])
            for yy in range(2):
                both = gu[g, hi, 1, 2 * i + yy].astype(F32) + gua[g, i, yy].astype(F32)
                gu[g, hi, 1, 2 * i + yy] = both.astype(BF)
            grad_send(1, g, 2 + i, gu.at[g, hi, 1], gur.at[g, i], dev)

    def down_second(g):
        for i in range(2):
            grad_wait(0, g, 2 + i, gdr.at[g, i])
        for hi in range(2):
            for p in range(2):
                total = gd[g, y, hi, p].astype(F32)
                for i in range(2):
                    total += gdr[g, i, hi, p].astype(F32)
                gds[g, hi, p] = total.astype(BF)
        for j in range(3):
            grad_send(2, g, j, gds.at[g, peer_hi[j], peer_p[j]], gdr2.at[g, j], x_peers[j])

    def up_second(g):
        for i in range(2):
            grad_wait(1, g, 2 + i, gur.at[g, i])
        for yy in range(4):
            total = gu[g, x_hi, 0, yy].astype(F32)
            for i in range(2):
                total += gur[g, i, yy].astype(F32)
            gus[g, yy] = total.astype(BF)
        for j in range(3):
            grad_send(3, g, j, gus.at[g, lax.rem(y + j + 1, 4)], gur2.at[g, j], y_peers[j])

    def down_last(g):
        for j in range(3):
            grad_wait(2, g, j, gdr2.at[g, j])
        total = gds[g, x_hi, 0].astype(F32)
        for j in range(3):
            total += gdr2[g, j].astype(F32)
        dg_out[g * PER:(g + 1) * PER] = total

    def up_last(g):
        for j in range(3):
            grad_wait(3, g, j, gur2.at[g, j])
        total = gus[g, y].astype(F32)
        for j in range(3):
            total += gur2[g, j].astype(F32)
        ug_out[g * PER:(g + 1) * PER] = total

    send_swapped(1)
    forward(0, 1)
    own_products(0, (0,))
    forward(1, 1)
    pass_weights(0)
    own_products(0, (1, 7))
    forward(0, 2)
    own_products(1, (0,))
    forward(1, 2)
    own_products(0, (2, 6))
    pass_weights(1)
    forward(0, 3)
    own_products(1, (1, 7))
    to_smem.wait()
    forward(1, 3)
    last_unit(0)
    own_products(0, (3, 5))
    rest_of_weights(0)
    own_products(0, (4,))
    other_products(0)
    gelu()
    turn()
    rest_of_weights(1)
    partial(0, 4)
    partial(0, 3)
    ring_first(0)
    own_products(1, (2, 6))
    partial(0, 5)
    accumulate(1, 1, 0, True)
    accumulate(1, 1, 1, False)
    accumulate(1, 1, 7, False)
    accumulate(1, 1, 2, False)
    accumulate(1, 1, 6, False)
    last_unit(1)
    own_products(1, (3, 5))
    accumulate(1, 1, 3, False)
    accumulate(1, 1, 5, False)
    sib_wait(1, 4)
    down_group(0)
    accumulate(1, 0, 4, False)
    accumulate(1, 1, 4, False)
    slopes()
    up_group(0)
    down_group(1)
    ring_step(0, 1)
    up_group(1)
    down_group(2)
    down_mid(0)
    up_mid(0)
    up_group(2)
    partial(1, 4)
    down_mid(1)
    up_mid(1)
    ring_first(1)
    partial(0, 2)
    partial(0, 6)
    down_mid(2)
    up_mid(2)
    ring_step(0, 2)
    partial(1, 3)
    partial(1, 5)
    ring_step(1, 1)
    down_second(0)
    up_second(0)
    partial(1, 2)
    partial(1, 6)
    partial(0, 1)
    partial(0, 7)
    ring_step(0, 3)
    down_second(1)
    up_second(1)
    ring_step(1, 2)
    partial(1, 1)
    partial(1, 7)
    partial(0, 0)
    down_second(2)
    up_second(2)
    ring_step(1, 3)
    partial(1, 0)
    ring_last(0)
    down_last(0)
    up_last(0)
    down_last(1)
    up_last(1)
    fin_last(0)
    ring_last(1)
    down_last(2)
    up_last(2)
    fin_last(1)
    for copy in started:
        copy.wait_send()


def hand_over(*refs):
    for i in range(4):
        refs[4 + i][...] = refs[i][...]


def local(
    tokens, cotangent, up_tiles, up_rows, up_columns, up_counts,
    down_tiles, down_rows, down_columns, down_counts,
):
    dma = pltpu.SemaphoreType.DMA
    vm = pltpu.VMEM
    any_space = pl.BlockSpec(memory_space=pl.ANY)
    in_vmem = pl.BlockSpec(memory_space=pltpu.VMEM)
    shapes = (
        jax.ShapeDtypeStruct((ROWS, HALF), BF),
        jax.ShapeDtypeStruct((ROWS, HALF), BF),
        jax.ShapeDtypeStruct((SLOTS, SLICE, BLK), F32),
        jax.ShapeDtypeStruct((SLOTS, SLICE, BLK), F32),
    )
    made = pl.pallas_call(
            kernel,
            out_shape=shapes,
            in_specs=[any_space] * 4 + [pl.BlockSpec(memory_space=pltpu.SMEM)] * 6,
            out_specs=(in_vmem,) * 4,
            scratch_shapes=[
                vm((2, 8, 2, 2, MY_ROWS, HALF), BF),
                vm((SLOTS, BLK, BLK), BF), vm((SLOTS, BLK, BLK), BF),
                vm((SLOTS, BLK, BLK), BF), vm((SLOTS, BLK, BLK), BF),
                vm((8, 128), jnp.int32), vm((8, 128), jnp.int32),
                pltpu.SMEM((2, 8, 128), jnp.int32),
                vm((4, MY_ROWS, BLK), F32),
                vm((4, MY_ROWS, BLK), F32),
                vm((4, MY_ROWS, BLK), BF),
                vm((4, MY_ROWS, BLK), BF),
                vm((8, 2, BLK, MY_ROWS), BF),
                vm((4, BLK, MY_ROWS), BF),
                vm((2, 8, 2, 2, MY_ROWS, HALF), BF),
                vm((2, 8, 2, MY_ROWS, HALF), BF),
                vm((2, 2, 4, 2, MY_ROWS, HALF), BF),
                vm((2, MY_ROWS, HALF), BF),
                vm((GROUPS, 4, 2, 2, PER, SLICE, BLK), BF),
                vm((GROUPS, 2, 2, PER, SLICE, BLK), BF),
                vm((GROUPS, 2, 2, 2, PER, SLICE, BLK), BF),
                vm((GROUPS, 2, 2, PER, SLICE, BLK), BF),
                vm((GROUPS, 3, PER, SLICE, BLK), BF),
                vm((GROUPS, 2, 2, 4, PER, SLICE, BLK), BF),
                vm((GROUPS, 2, 2, PER, SLICE, BLK), BF),
                vm((GROUPS, 2, 4, PER, SLICE, BLK), BF),
                vm((GROUPS, 4, PER, SLICE, BLK), BF),
                vm((GROUPS, 3, PER, SLICE, BLK), BF),
                dma((6,)),
                dma((3,)), dma((3,)),
                dma((2, 2, 4, 2)), dma((2, 2, 4, 2)),
                dma((2, 8)), dma((2, 8)),
                dma((2, 4)), dma((2, 4)),
                dma((2, 8)), dma((2, 8)),
                dma((2, 2, 4, 2)), dma((2, 2, 4, 2)),
                dma((2,)), dma((2,)),
                dma((4, GROUPS, 4)), dma((4, GROUPS, 4)),
            ],
            compiler_params=pltpu.CompilerParams(
                collective_id=0, has_side_effects=True, vmem_limit_bytes=58 << 20
            ),
            name="sparse_feed_forward",
        )(
        tokens, cotangent, up_tiles, down_tiles, up_rows, up_columns, up_counts,
        down_rows, down_columns, down_counts,
    )
    return tuple(
        pl.pallas_call(
            hand_over,
            out_shape=shapes,
            in_specs=[in_vmem] * 4,
            out_specs=(in_vmem,) * 4,
            name="hand_over",
        )(*made)
    )


def solution(mesh):
    return jax.shard_map(
        local,
        mesh=mesh,
        in_specs=(
            P("dp", "mp"),
            P("dp", "mp"),
            P("mp", None, None),
            P("mp"),
            P("mp"),
            P("mp"),
            P("mp", None, None),
            P("mp"),
            P("mp"),
            P("mp"),
        ),
        out_specs=(P("dp", "mp"), P("dp", "mp"), P("mp", "dp", None), P("mp", "dp", None)),
        check_vma=False,
    )
```
